32 devices in a mesh: ctx: 8 (over y, x, core), wsh: 4 (over z).
Axes of the slice: x: 2, y: 2, z: 4, core: 2. Of those that a mesh axis runs over, the one named last changes fastest.
Arguments:
- tokens: bfloat16 [8, 1024, 768], P('wsh', 'ctx'), may hold values from -6 to 6
- key_mask: int32 [8, 1024], P('wsh', 'ctx'), may hold values from 0 to 1, as said below
- w_qkv: bfloat16 [768, 2304], P('wsh'), may hold values from -0.3125 to 0.3125
- w_attn_out: bfloat16 [768, 768], P('wsh'), may hold values from -0.5 to 0.5
- w_in: bfloat16 [768, 2304], P('wsh'), may hold values from -0.21875 to 0.21875
- w_out: bfloat16 [1152, 768], P('wsh'), may hold values from -0.1875 to 0.1875
- attn_gain: bfloat16 [768], P('wsh'), may hold values from 0.099609375 to 1.8984375
- mlp_gain: bfloat16 [768], P('wsh'), may hold values from 0.099609375 to 1.8984375
- cotangent: bfloat16 [8, 1024, 768], P('wsh', 'ctx'), may hold values from -6 to 6
Outputs:
- output: bfloat16 [8, 1024, 768], P('wsh', 'ctx')
- grad_tokens: bfloat16 [8, 1024, 768], P('wsh', 'ctx')
- attn_gain_grad: float32 [768], P('wsh')
- mlp_gain_grad: float32 [768], P('wsh')
- w_qkv_grad: float32 [768, 2304], P('wsh')
- w_attn_out_grad: float32 [768, 768], P('wsh')
- w_in_grad: float32 [768, 2304], P('wsh')
- w_out_grad: float32 [1152, 768], P('wsh')
The draws below stay inside these ranges and needn't reach their ends.
Inputs may be any that keep to these rules, and one draw needn't show every extreme that they name: `key_mask`: in each sequence the ones form a prefix that ends within the last 128 positions, and the last position is 0.
All inputs are finite; a program needn't handle non-finite values.
Results may differ from the reference program's by a relative error of at most 0.02.
Values may be sent and summed in bfloat16 or wider, within the bound.
A program may use at most 256 MiB of HBM per device.

```python
import math
import jax
import jax.numpy as jnp
from jax import lax

D = 768
HEADS = 12
HEAD_DIM = 64
FF = 1152
TOK_DEV = 128
LEN = 1024
SEQS = 8


def draw_key_mask(key, part):
    key = jax.random.fold_in(key, 11)
    ends = jax.random.randint(key, (SEQS, 1), LEN - TOK_DEV + 1, LEN)
    return (jnp.arange(LEN, dtype=jnp.int32)[None, :] < ends).astype(jnp.int32)


def levels(key, extent, pieces, low, top_value):
    def one(position, parts):
        draws = jax.random.uniform(jax.random.fold_in(jax.random.fold_in(key, 6), position), (parts,), jnp.float32, low / len(pieces), top_value / len(pieces))
        return jnp.repeat(jnp.exp(draws), extent[position] // parts).reshape((-1,) + (1,) * (len(extent) - position - 1))

    factor_of = one(*pieces[0])
    for cut in pieces[1:]:
        factor_of = factor_of * one(*cut)
    return factor_of


def gaussian(stream_key, shape, width, limit, split=(), kind=jnp.bfloat16):
    entries = width * jax.random.normal(stream_key, shape, jnp.float32)
    if split:
        entries = entries * levels(stream_key, shape, split, -0.22, 0.18)
    return jnp.clip(entries, -limit, limit).astype(kind)


def setup_inputs(seed: int = 0) -> dict:
    keys = jax.random.split(jax.random.key(seed), 10)
    tokens = gaussian(keys[0], (SEQS, LEN, D), 1.0, 6.0, ((0, 4), (1, 8)))
    key_mask = draw_key_mask(jax.random.fold_in(keys[9], 71), 0)
    w_qkv = gaussian(keys[2], (D, 3 * D), (D // 2) ** -0.5, 0.3125, ((0, 4),))
    w_attn_out = gaussian(keys[3], (D, D), (max(1, D * 160 // LEN)) ** -0.5, 0.5, ((0, 4),))
    w_in = gaussian(keys[4], (D, 2 * FF), D ** -0.5, 0.21875, ((0, 4),))
    w_out = gaussian(keys[5], (FF, D), FF ** -0.5, 0.1875, ((0, 4),))
    attn_gain = jnp.clip(1.0 + 0.18 * jax.random.normal(keys[6], (D,), jnp.float32), 0.099609375, 1.8984375).astype(jnp.bfloat16)
    mlp_gain = jnp.clip(1.0 + 0.18 * jax.random.normal(keys[7], (D,), jnp.float32), 0.099609375, 1.8984375).astype(jnp.bfloat16)
    cotangent = gaussian(keys[8], (SEQS, LEN, D), 1.0, 6.0, ((0, 4), (1, 8)))
    return {"tokens": tokens, "key_mask": key_mask, "w_qkv": w_qkv, "w_attn_out": w_attn_out, "w_in": w_in, "w_out": w_out, "attn_gain": attn_gain, "mlp_gain": mlp_gain, "cotangent": cotangent}


@jax.custom_vjp
def low(v):
    return lax.optimization_barrier(v.astype(jnp.bfloat16)).astype(jnp.float32)

@jax.custom_vjp
def low_back(v):
    return v

def low_keep(v):
    return (low(v), None)

def low_pass(kept, grad):
    return (grad,)

def back_keep(v):
    return (v, None)

def back_low(kept, grad):
    return (low(grad),)
low.defvjp(low_keep, low_pass)
low_back.defvjp(back_keep, back_low)
EPSILON = 1e-05
THETA = 160000.0
MASKED = -1e+30
HIGHEST = lax.Precision.HIGHEST

def layer_norm(values, gain):
    centred = values - lax.optimization_barrier(jnp.mean(values, axis=-1, keepdims=True))
    spread = lax.optimization_barrier(jnp.mean(centred * centred, axis=-1, keepdims=True))
    return centred * lax.rsqrt(spread + EPSILON) * gain

def rotary(heads_in, positions):
    half_dim = heads_in.shape[-1] // 2
    counter = jnp.arange(half_dim, dtype=jnp.float32)
    inverse = jnp.exp(counter * (-2.0 * math.log(THETA) / heads_in.shape[-1]))
    angles = positions.astype(jnp.float32)[:, None] * inverse[None, :]
    cosine = jnp.cos(angles)[:, None, :]
    sine_part = jnp.sin(angles)[:, None, :]
    first_half = heads_in[..., :half_dim]
    second = heads_in[..., half_dim:]
    return jnp.concatenate([first_half * cosine - second * sine_part, second * cosine + first_half * sine_part], axis=-1)

def geglu(projected):
    half_width = projected.shape[-1] // 2
    inner_part = projected[:, :half_width]
    gating = projected[:, half_width:]
    return 0.5 * inner_part * (1.0 + lax.erf(inner_part * 0.5 ** 0.5)) * gating

def attend_block(query_block, key_rows, value_rows, is_valid):
    raw_scores = jnp.einsum('qhd,khd->hqk', query_block, key_rows, precision=HIGHEST) * HEAD_DIM ** (-0.5)
    scores = jnp.where(is_valid[None, None, :], low_back(raw_scores), MASKED)
    row_top = lax.optimization_barrier(jnp.max(scores, axis=-1, keepdims=True))
    weights = jnp.exp(scores - row_top)
    probability = weights / lax.optimization_barrier(jnp.sum(weights, axis=-1, keepdims=True))
    return jnp.einsum('hqk,khd->qhd', low(probability), value_rows, precision=HIGHEST)

def layer(seq_tokens, is_valid, w_qkv, w_attn_out, w_in, w_out, attn_gain, mlp_gain):
    length = seq_tokens.shape[0]
    positions = jnp.arange(length, dtype=jnp.int32)
    normed = low(layer_norm(seq_tokens, attn_gain))
    joined_proj = low_back(jnp.dot(normed, w_qkv, precision=HIGHEST))
    shaped = (length, HEADS, HEAD_DIM)
    queries = low(rotary(joined_proj[:, :D].reshape(shaped), positions))
    key_rows = low(rotary(joined_proj[:, D:2 * D].reshape(shaped), positions))
    value_rows = low(joined_proj[:, 2 * D:].reshape(shaped))
    block_len = math.gcd(length, 512)
    grouped = queries.reshape(length // block_len, block_len, HEADS, HEAD_DIM)
    attend = jax.checkpoint(lambda query_block: attend_block(query_block, key_rows, value_rows, is_valid))
    mixed_heads = lax.map(attend, grouped).reshape(length, D)
    attended = low(low_back(mixed_heads))
    hidden = seq_tokens + low_back(jnp.dot(attended, w_attn_out, precision=HIGHEST))
    normed_two = low(layer_norm(hidden, mlp_gain))
    projected = low_back(jnp.dot(normed_two, w_in, precision=HIGHEST))
    gated = low(geglu(projected))
    return hidden + low_back(jnp.dot(gated, w_out, precision=HIGHEST))

def reference(tokens, key_mask, w_qkv, w_attn_out, w_in, w_out, attn_gain, mlp_gain, cotangent):
    params = tuple((member.astype(jnp.float32) for member in (w_qkv, w_attn_out, w_in, w_out, attn_gain, mlp_gain)))

    def per_sequence(grad_total, inputs_now):
        seq_tokens, seq_mask, seq_cot = inputs_now
        is_valid = seq_mask > 0

        def forward(seq_in, *weights_in):
            return layer(seq_in, is_valid, *weights_in)
        result, pullback = jax.vjp(forward, seq_tokens.astype(jnp.float32), *params)
        gradients = pullback(seq_cot.astype(jnp.float32))
        grad_total = tuple((summed + gradient for summed, gradient in zip(grad_total, gradients[1:])))
        return (grad_total, (result.astype(jnp.bfloat16), gradients[0].astype(jnp.bfloat16)))
    starting = tuple((jnp.zeros(member.shape, jnp.float32) for member in params))
    totals, (outputs, grad_tokens) = lax.scan(per_sequence, starting, (tokens, key_mask, cotangent))
    return (outputs, grad_tokens, totals[4], totals[5], totals[0], totals[1], totals[2], totals[3])
```

```python
import math

import jax
import jax.numpy as jnp
from jax import lax
from jax.experimental import pallas as pl
from jax.experimental.pallas import tpu as pltpu
from jax.sharding import PartitionSpec as P

HEADS = 12


EPSILON = 1e-05
THETA = 160000.0
MASKED = -1e30


def layer_norm(values, gain):
    centred = values - jnp.mean(values, axis=-1, keepdims=True)
    spread = jnp.mean(centred * centred, axis=-1, keepdims=True)
    return centred * lax.rsqrt(spread + EPSILON) * gain


def rotary(heads_in, positions):
    half_dim = heads_in.shape[-1] // 2
    counter = jnp.arange(half_dim, dtype=jnp.float32)
    inverse = jnp.exp(counter * (-2.0 * math.log(THETA) / heads_in.shape[-1]))
    angles = positions.astype(jnp.float32)[:, None] * inverse[None, :]
    cosine = jnp.cos(angles)[:, None, :]
    sine_part = jnp.sin(angles)[:, None, :]
    first_half = heads_in[..., :half_dim]
    second = heads_in[..., half_dim:]
    return jnp.concatenate(
        [first_half * cosine - second * sine_part, second * cosine + first_half * sine_part],
        axis=-1,
    )


def geglu(projected):
    half_width = projected.shape[-1] // 2
    inner_part = projected[:, :half_width]
    gating = projected[:, half_width:]
    return 0.5 * inner_part * (1.0 + lax.erf(inner_part * 0.5**0.5)) * gating


def by_positions(tokens, key_mask, w_qkv, w_attn_out, w_in, w_out, attn_gain, mlp_gain, cotangent):
    seq_here, row_count, width_all = tokens.shape
    head_count = HEADS
    head_width = width_all // head_count
    scaling = head_width ** (-0.5)
    seq_len = row_count * lax.axis_size("ctx")
    block_len = math.gcd(seq_len, 1024)
    num_blocks = seq_len // block_len
    all_rows = seq_here * row_count
    per_head = (all_rows, head_count, head_width)

    def heads_first(rows):
        return jnp.transpose(
            rows.reshape(seq_here, row_count, head_count, head_width), (0, 2, 1, 3)
        )

    def heads_last(rows):
        return jnp.transpose(
            rows.reshape(seq_here, row_count, head_count, head_width), (0, 2, 3, 1)
        )

    def rows_from_first(stacked):
        return jnp.transpose(stacked, (0, 2, 1, 3)).reshape(per_head)

    def rows_from_last(stacked):
        return jnp.transpose(stacked, (0, 3, 1, 2)).reshape(per_head)

    full_qkv, full_attn, full_in, full_out, gain_one, gain_two = (
        lax.all_gather(w_qkv, "wsh", axis=0, tiled=True),
        lax.all_gather(w_attn_out, "wsh", axis=0, tiled=True),
        lax.all_gather(w_in, "wsh", axis=0, tiled=True),
        lax.all_gather(w_out, "wsh", axis=0, tiled=True),
        lax.all_gather(attn_gain, "wsh", axis=0, tiled=True),
        lax.all_gather(mlp_gain, "wsh", axis=0, tiled=True),
    )
    residual_in = tokens.reshape(all_rows, width_all).astype(jnp.float32)
    local_pos = lax.axis_index("ctx") * row_count + jnp.arange(row_count, dtype=jnp.int32)
    positions = jnp.tile(local_pos, seq_here)
    normed_f, norm_one_pull = jax.vjp(layer_norm, residual_in, gain_one.astype(jnp.float32))
    normed = normed_f.astype(jnp.bfloat16)
    joined_proj = jnp.dot(normed, full_qkv, preferred_element_type=jnp.float32)

    def rotate_pair(query_part, key_part):
        return (
            rotary(query_part.reshape(per_head), positions),
            rotary(key_part.reshape(per_head), positions),
        )

    (query_f, key_f), rotate_pull = jax.vjp(
        rotate_pair, joined_proj[:, :width_all], joined_proj[:, width_all : 2 * width_all]
    )
    query_rows_low = query_f.astype(jnp.bfloat16)
    queries = heads_first(query_rows_low)
    keys_own = heads_last(key_f.astype(jnp.bfloat16))
    values_own = heads_last(joined_proj[:, 2 * width_all :].astype(jnp.bfloat16))
    mask_own = key_mask.astype(jnp.bfloat16).reshape(seq_here, 1, 1, row_count)
    keys_all, values_all, mask_all = (
        lax.all_gather(keys_own, "ctx", axis=3, tiled=True),
        lax.all_gather(values_own, "ctx", axis=3, tiled=True),
        lax.all_gather(mask_own, "ctx", axis=3, tiled=True),
    )

    def remote_block(index):
        start = index * block_len
        return (
            lax.dynamic_slice_in_dim(keys_all, start, block_len, 3),
            lax.dynamic_slice_in_dim(values_all, start, block_len, 3),
            lax.dynamic_slice_in_dim(mask_all, start, block_len, 3),
        )

    def forward_step(carried, index):
        running_top, running_total, running_sum = carried
        key_block, value_block, mask_block = remote_block(index)
        raw_scores = (
            jnp.einsum("bhqd,bhdk->bhqk", queries, key_block, preferred_element_type=jnp.float32)
            * scaling
        )
        scores = jnp.where(mask_block > 0.5, raw_scores, MASKED)
        new_top = jnp.maximum(running_top, jnp.max(scores, axis=-1))
        fade_factor = jnp.exp(running_top - new_top)
        weights = jnp.exp(scores - new_top[..., None])
        running_total = running_total * fade_factor + jnp.sum(weights, axis=-1)
        running_sum = running_sum * fade_factor[..., None] + jnp.einsum(
            "bhqk,bhdk->bhqd",
            weights.astype(jnp.bfloat16),
            value_block,
            preferred_element_type=jnp.float32,
        )
        return ((new_top, running_total, running_sum), None)

    stat_shape = (seq_here, head_count, row_count)
    block_ids = jnp.arange(num_blocks, dtype=jnp.int32)
    start_state = (
        jnp.full(stat_shape, MASKED, jnp.float32),
        jnp.zeros(stat_shape, jnp.float32),
        jnp.zeros(stat_shape + (head_width,), jnp.float32),
    )
    (final_top, final_total, final_sum), unused_out = lax.scan(forward_step, start_state, block_ids)
    log_total = final_top + jnp.log(final_total)
    attended_heads = final_sum / final_total[..., None]
    attended = rows_from_first(attended_heads).reshape(all_rows, width_all).astype(jnp.bfloat16)
    hidden = residual_in + jnp.dot(attended, full_attn, preferred_element_type=jnp.float32)
    normed_two_f, norm_two_pull = jax.vjp(layer_norm, hidden, gain_two.astype(jnp.float32))
    normed_two = normed_two_f.astype(jnp.bfloat16)
    projected = jnp.dot(normed_two, full_in, preferred_element_type=jnp.float32)
    gated_f, glu_pull = jax.vjp(geglu, projected)
    gated = gated_f.astype(jnp.bfloat16)
    result = hidden + jnp.dot(gated, full_out, preferred_element_type=jnp.float32)
    outcome = result.astype(jnp.bfloat16).reshape(seq_here, row_count, width_all)
    grad_out = cotangent.reshape(all_rows, width_all)
    grad_w_out = jnp.dot(gated.T, grad_out, preferred_element_type=jnp.float32)
    grad_gated = jnp.dot(grad_out, full_out.T, preferred_element_type=jnp.float32)
    (grad_proj,) = glu_pull(grad_gated)
    grad_proj_low = grad_proj.astype(jnp.bfloat16)
    grad_w_in = jnp.dot(normed_two.T, grad_proj_low, preferred_element_type=jnp.float32)
    grad_norm_two = jnp.dot(grad_proj_low, full_in.T, preferred_element_type=jnp.float32)
    grad_hidden_ln, grad_gain_two = norm_two_pull(grad_norm_two)
    grad_hidden = grad_out.astype(jnp.float32) + grad_hidden_ln
    grad_branch = grad_hidden.astype(jnp.bfloat16)
    grad_w_attn = jnp.dot(attended.T, grad_branch, preferred_element_type=jnp.float32)
    grad_att_rows = (
        jnp.dot(grad_branch, full_attn.T, preferred_element_type=jnp.float32)
        .astype(jnp.bfloat16)
        .reshape(per_head)
    )
    grad_attended = heads_first(grad_att_rows)
    delta_heads = jnp.sum(grad_attended.astype(jnp.float32) * attended_heads, axis=-1)

    def remote_terms(index):
        key_block, value_block, mask_block = remote_block(index)
        raw_scores = (
            jnp.einsum("bhqd,bhdk->bhqk", queries, key_block, preferred_element_type=jnp.float32)
            * scaling
        )
        scores = jnp.where(mask_block > 0.5, raw_scores, MASKED)
        probability = jnp.exp(scores - log_total[..., None])
        grad_probs = jnp.einsum(
            "bhqd,bhdk->bhqk", grad_attended, value_block, preferred_element_type=jnp.float32
        )
        grad_scores = (probability * (grad_probs - delta_heads[..., None])).astype(jnp.bfloat16)
        grad_query_part = (
            jnp.einsum(
                "bhqk,bhdk->bhqd", grad_scores, key_block, preferred_element_type=jnp.float32
            )
            * scaling
        )
        return (probability, grad_scores, grad_query_part)

    whole_zeros = jnp.zeros((seq_here, head_count, head_width, seq_len), jnp.float32)

    def key_step(carried, index):
        grad_query_acc, key_terms, value_terms = carried
        probability, grad_scores, grad_query_part = remote_terms(index)
        grad_value_block = jnp.einsum(
            "bhqk,bhqd->bhdk",
            probability.astype(jnp.bfloat16),
            grad_attended,
            preferred_element_type=jnp.float32,
        )
        grad_key_block = (
            jnp.einsum("bhqk,bhqd->bhdk", grad_scores, queries, preferred_element_type=jnp.float32)
            * scaling
        )
        start = index * block_len
        key_terms = lax.dynamic_update_slice_in_dim(key_terms, grad_key_block, start, 3)
        value_terms = lax.dynamic_update_slice_in_dim(value_terms, grad_value_block, start, 3)
        return ((grad_query_acc + grad_query_part, key_terms, value_terms), None)

    (grad_query_heads, key_terms, value_terms), unused_steps = lax.scan(
        key_step,
        (jnp.zeros(stat_shape + (head_width,), jnp.float32), whole_zeros, whole_zeros),
        block_ids,
    )
    grad_key_heads, grad_value_heads = (
        lax.psum_scatter(key_terms, "ctx", scatter_dimension=3, tiled=True),
        lax.psum_scatter(value_terms, "ctx", scatter_dimension=3, tiled=True),
    )
    grad_query = rows_from_first(grad_query_heads)
    grad_key = rows_from_last(grad_key_heads)
    grad_value = rows_from_last(grad_value_heads)
    grad_query_pre, grad_key_pre = rotate_pull((grad_query, grad_key))
    grad_joined = jnp.concatenate(
        [grad_query_pre, grad_key_pre, grad_value.reshape(all_rows, width_all)], axis=1
    ).astype(jnp.bfloat16)
    grad_w_qkv = jnp.dot(normed.T, grad_joined, preferred_element_type=jnp.float32)
    grad_normed = jnp.dot(grad_joined, full_qkv.T, preferred_element_type=jnp.float32)
    grad_in_ln, grad_gain_one = norm_one_pull(grad_normed)
    grad_tokens = (
        (grad_hidden + grad_in_ln).astype(jnp.bfloat16).reshape(seq_here, row_count, width_all)
    )
    every_part = (
        lax.psum_scatter(
            grad_w_qkv.astype(jnp.bfloat16), "wsh", scatter_dimension=0, tiled=True
        ).astype(jnp.float32),
        lax.psum_scatter(
            grad_w_attn.astype(jnp.bfloat16), "wsh", scatter_dimension=0, tiled=True
        ).astype(jnp.float32),
        lax.psum_scatter(
            grad_w_in.astype(jnp.bfloat16), "wsh", scatter_dimension=0, tiled=True
        ).astype(jnp.float32),
        lax.psum_scatter(
            grad_w_out.astype(jnp.bfloat16), "wsh", scatter_dimension=0, tiled=True
        ).astype(jnp.float32),
        lax.psum_scatter(
            grad_gain_one.astype(jnp.bfloat16), "wsh", scatter_dimension=0, tiled=True
        ).astype(jnp.float32),
        lax.psum_scatter(
            grad_gain_two.astype(jnp.bfloat16), "wsh", scatter_dimension=0, tiled=True
        ).astype(jnp.float32),
    )
    sum_qkv, sum_attn, sum_in, sum_out, sum_gain_one, sum_gain_two = lax.psum(
        (every_part[0], every_part[1], every_part[2], every_part[3], every_part[4], every_part[5]),
        "ctx",
    )
    return (outcome, grad_tokens, sum_gain_one, sum_gain_two, sum_qkv, sum_attn, sum_in, sum_out)


NT = (((1,), (1,)), ((), ()))
NN = (((1,), (0,)), ((), ()))
TN = (((0,), (0,)), ((), ()))


def mm(left, right, dims=NN):
    return lax.dot_general(left, right, dims, preferred_element_type=jnp.float32)


def attend_kernel(q_ref, k_ref, v_ref, mask_ref, o_ref, p_ref):
    width = q_ref.shape[1]
    scores = mm(k_ref[0], q_ref[0], TN) * width ** (-0.5)
    scores = jnp.where(mask_ref[...] > 0.5, scores, MASKED)
    top = jnp.max(scores, axis=0, keepdims=True)
    weights = jnp.exp(scores - top)
    prob = weights * (1.0 / jnp.sum(weights, axis=0, keepdims=True))
    p_ref[0] = prob
    o_ref[0] = mm(v_ref[0], prob.astype(jnp.bfloat16))


def attend(queries, keys, values, mask_col):
    pairs, width, length = queries.shape
    rows = math.gcd(length, 256)
    one = lambda: pl.BlockSpec((1, width, length), lambda i, j: (i, 0, 0))
    part = lambda: pl.BlockSpec((1, width, rows), lambda i, j: (i, 0, j))
    return pl.pallas_call(
        attend_kernel,
        grid=(pairs, length // rows),
        in_specs=[part(), one(), one(), pl.BlockSpec((length, 1), lambda i, j: (0, 0))],
        out_specs=[part(), pl.BlockSpec((1, length, rows), lambda i, j: (i, 0, j))],
        out_shape=[
            jax.ShapeDtypeStruct((pairs, width, length), jnp.float32),
            jax.ShapeDtypeStruct((pairs, length, length), jnp.float32),
        ],
        compiler_params=pltpu.CompilerParams(vmem_limit_bytes=40 * 2**20),
        cost_estimate=pl.CostEstimate(
            flops=4 * pairs * width * length**2,
            bytes_accessed=4 * pairs * length**2,
            transcendentals=pairs * length**2,
        ),
    )(queries, keys, values, mask_col)


def attend_back_kernel(q_ref, k_ref, v_ref, do_ref, o_ref, p_ref, dq_ref, dk_ref, dv_ref):
    step = pl.program_id(1)
    scaling = q_ref.shape[1] ** (-0.5)
    grad_out = do_ref[0]
    delta = jnp.sum(grad_out.astype(jnp.float32) * o_ref[0], axis=0, keepdims=True)
    prob = p_ref[0]
    grad_prob = mm(v_ref[0], grad_out, TN)
    grad_scores = (prob * (grad_prob - delta)).astype(jnp.bfloat16)
    dq_ref[0] = mm(k_ref[0], grad_scores) * scaling

    @pl.when(step == 0)
    def _():
        dk_ref[...] = jnp.zeros_like(dk_ref)
        dv_ref[...] = jnp.zeros_like(dv_ref)

    dk_ref[0] += mm(q_ref[0], grad_scores, NT) * scaling
    dv_ref[0] += mm(grad_out, prob.astype(jnp.bfloat16), NT)


def attend_back(queries, keys, values, grad_out, mixed, prob):
    pairs, width, length = queries.shape
    rows = math.gcd(length, 256)
    one = lambda: pl.BlockSpec((1, width, length), lambda i, j: (i, 0, 0))
    part = lambda: pl.BlockSpec((1, width, rows), lambda i, j: (i, 0, j))
    shape = jax.ShapeDtypeStruct((pairs, width, length), jnp.float32)
    return pl.pallas_call(
        attend_back_kernel,
        grid=(pairs, length // rows),
        in_specs=[
            part(),
            one(),
            one(),
            part(),
            part(),
            pl.BlockSpec((1, length, rows), lambda i, j: (i, 0, j)),
        ],
        out_specs=[part(), one(), one()],
        out_shape=[shape, shape, shape],
        compiler_params=pltpu.CompilerParams(vmem_limit_bytes=40 * 2**20),
        cost_estimate=pl.CostEstimate(
            flops=8 * pairs * width * length**2,
            bytes_accessed=4 * pairs * length**2,
            transcendentals=0,
        ),
    )(queries, keys, values, grad_out, mixed, prob)


def gather_rows(part):
    pieces = lax.axis_size("ctx")
    rows = part.shape[0] // pieces
    mine = lax.dynamic_slice_in_dim(part, lax.axis_index("ctx") * rows, rows, 0)
    return lax.all_gather(mine, ("wsh", "ctx"), axis=0, tiled=True)


def sum_rows(term):
    total, width = term.shape
    fold = 2 if total % 256 else 1
    term = term.astype(jnp.bfloat16).reshape(total * fold, width // fold)
    piece = lax.psum_scatter(term, ("wsh", "ctx"), scatter_dimension=0, tiled=True)
    sums = lax.all_gather(piece, "ctx", axis=0, tiled=True)
    return sums.reshape(-1, width).astype(jnp.float32)


def by_heads(tokens, key_mask, w_qkv, w_attn_out, w_in, w_out, attn_gain, mlp_gain, cotangent):
    seqs, rows, width = tokens.shape
    peers = lax.axis_size("ctx")
    head_width = width // HEADS
    half = head_width // 2
    pairs = seqs * HEADS // peers
    splits = peers // seqs
    feats = pairs * head_width
    length = rows * peers
    tokens_here = seqs * rows
    low = jnp.bfloat16

    gains = lax.all_gather(jnp.stack([attn_gain, mlp_gain]), "wsh", axis=1, tiled=True)
    gain_one, gain_two = gains[0], gains[1]
    full_qkv = gather_rows(w_qkv)
    full_attn = gather_rows(w_attn_out)
    full_in = gather_rows(w_in)
    full_out = gather_rows(w_out)

    def to_heads(parts):
        count = parts.shape[0]
        sent = jnp.transpose(
            parts.reshape(count, splits, feats, seqs, rows), (3, 1, 0, 2, 4)
        ).reshape(peers, count * feats, rows)
        return sent

    def swap(sent):
        return lax.all_to_all(sent, "ctx", split_axis=0, concat_axis=0, tiled=True)

    def to_rows(parts):
        count = parts.shape[0]
        sent = jnp.transpose(
            parts.astype(low).reshape(count * feats, peers, rows), (1, 0, 2)
        )
        got = swap(sent).reshape(seqs, splits, count, feats, rows)
        return jnp.transpose(got, (2, 1, 3, 0, 4)).reshape(count, width, tokens_here)

    residual_in = tokens.reshape(tokens_here, width).astype(jnp.float32)
    normed_f, norm_one_pull = jax.vjp(layer_norm, residual_in, gain_one.astype(jnp.float32))
    normed = normed_f.astype(low)
    joined = mm(full_qkv, normed, (((0,), (1,)), ((), ())))

    local_pos = lax.axis_index("ctx") * rows + jnp.arange(rows, dtype=jnp.int32)
    inverse = jnp.exp(
        jnp.arange(half, dtype=jnp.float32) * (-2.0 * math.log(THETA) / head_width)
    )
    angles = inverse[:, None] * jnp.tile(local_pos, seqs).astype(jnp.float32)[None, :]
    cosine, sine = jnp.cos(angles), jnp.sin(angles)

    def turn(values, way):
        pair = values.reshape(HEADS, 2, half, tokens_here)
        first, second = pair[:, 0], pair[:, 1]
        return jnp.stack(
            [first * cosine - way * (second * sine), second * cosine + way * (first * sine)], axis=1
        ).reshape(width, tokens_here)

    trio = jnp.stack(
        [turn(joined[:width], 1.0), turn(joined[width : 2 * width], 1.0), joined[2 * width :]]
    ).astype(low)
    mask_rows = jnp.broadcast_to(
        key_mask.astype(low)[:, None, None, :], (seqs, splits, 16, rows)
    ).reshape(peers, 16, rows)
    got = swap(jnp.concatenate([to_heads(trio), mask_rows], axis=1))
    got = jnp.transpose(got, (1, 0, 2)).reshape(3 * feats + 16, length)
    queries, keys, values = (
        got[i * feats : (i + 1) * feats].reshape(pairs, head_width, length) for i in range(3)
    )
    mask_col = got[3 * feats].astype(jnp.float32)[:, None]
    mixed, prob = attend(queries, keys, values, mask_col)
    attended = jnp.transpose(to_rows(mixed.reshape(1, feats, length))[0])

    hidden = residual_in + mm(attended, full_attn)
    normed_two_f, norm_two_pull = jax.vjp(layer_norm, hidden, gain_two.astype(jnp.float32))
    normed_two = normed_two_f.astype(low)
    projected = mm(normed_two, full_in)
    gated_f, glu_pull = jax.vjp(geglu, projected)
    gated = gated_f.astype(low)
    outcome = (hidden + mm(gated, full_out)).astype(low).reshape(seqs, rows, width)
    grad_out = cotangent.reshape(tokens_here, width)
    grad_w_out = sum_rows(mm(gated, grad_out, TN))
    (grad_proj,) = glu_pull(mm(grad_out, full_out, NT))
    grad_proj = grad_proj.astype(low)
    grad_w_in = sum_rows(mm(normed_two, grad_proj, TN))
    grad_hidden_ln, grad_gain_two = norm_two_pull(mm(grad_proj, full_in, NT))
    grad_hidden = grad_out.astype(jnp.float32) + grad_hidden_ln
    grad_branch = grad_hidden.astype(low)
    grad_w_attn = sum_rows(mm(attended, grad_branch, TN))
    grad_att = mm(full_attn, grad_branch, NT).astype(low)
    got_do = swap(to_heads(grad_att[None]))
    got_do = jnp.transpose(got_do, (1, 0, 2)).reshape(pairs, head_width, length)
    grads = attend_back(queries, keys, values, got_do, mixed, prob)
    back = to_rows(jnp.stack([g.reshape(feats, length) for g in grads])).astype(jnp.float32)
    grad_joined = jnp.concatenate([turn(back[0], -1.0), turn(back[1], -1.0), back[2]]).astype(low)
    grad_w_qkv = sum_rows(mm(normed, grad_joined, (((0,), (1,)), ((), ()))))
    grad_normed = mm(grad_joined, full_qkv, (((0,), (1,)), ((), ())))
    grad_in_ln, grad_gain_one = norm_one_pull(grad_normed)
    grad_tokens = (grad_hidden + grad_in_ln).astype(low).reshape(seqs, rows, width)
    gain_sums = lax.psum(jnp.stack([grad_gain_one, grad_gain_two]), ("ctx", "wsh"))
    share = attn_gain.shape[0]
    gain_sums = lax.dynamic_slice_in_dim(gain_sums, lax.axis_index("wsh") * share, share, 1)
    return (
        outcome,
        grad_tokens,
        gain_sums[0],
        gain_sums[1],
        grad_w_qkv,
        grad_w_attn,
        grad_w_in,
        grad_w_out,
    )


def shards(*arrays):
    seqs = arrays[0].shape[0]
    peers = lax.axis_size("ctx")
    even = (seqs * HEADS) % peers == 0 and peers % seqs == 0
    even = even and all(w.shape[0] % peers == 0 for w in arrays[2:6])
    return (by_heads if even else by_positions)(*arrays)


def solution(mesh):
    return jax.shard_map(
        shards,
        mesh=mesh,
        in_specs=(
            P("wsh", "ctx", None),
            P("wsh", "ctx"),
            P("wsh", None),
            P("wsh", None),
            P("wsh", None),
            P("wsh", None),
            P("wsh"),
            P("wsh"),
            P("wsh", "ctx", None),
        ),
        out_specs=(
            P("wsh", "ctx", None),
            P("wsh", "ctx", None),
            P("wsh"),
            P("wsh"),
            P("wsh", None),
            P("wsh", None),
            P("wsh", None),
            P("wsh", None),
        ),
        check_vma=False,
    )
```

```python
import functools
import math

import jax
import jax.numpy as jnp
from jax import lax
from jax.experimental import pallas as pl
from jax.experimental.pallas import tpu as pltpu
from jax.sharding import PartitionSpec as P

HEADS = 12


EPSILON = 1e-05
THETA = 160000.0
MASKED = -1e30


def layer_norm(values, gain):
    centred = values - jnp.mean(values, axis=-1, keepdims=True)
    spread = jnp.mean(centred * centred, axis=-1, keepdims=True)
    return centred * lax.rsqrt(spread + EPSILON) * gain


def rotary(heads_in, positions):
    half_dim = heads_in.shape[-1] // 2
    counter = jnp.arange(half_dim, dtype=jnp.float32)
    inverse = jnp.exp(counter * (-2.0 * math.log(THETA) / heads_in.shape[-1]))
    angles = positions.astype(jnp.float32)[:, None] * inverse[None, :]
    cosine = jnp.cos(angles)[:, None, :]
    sine_part = jnp.sin(angles)[:, None, :]
    first_half = heads_in[..., :half_dim]
    second = heads_in[..., half_dim:]
    return jnp.concatenate(
        [first_half * cosine - second * sine_part, second * cosine + first_half * sine_part],
        axis=-1,
    )


def geglu(projected):
    half_width = projected.shape[-1] // 2
    inner_part = projected[:, :half_width]
    gating = projected[:, half_width:]
    return 0.5 * inner_part * (1.0 + lax.erf(inner_part * 0.5**0.5)) * gating


def by_positions(tokens, key_mask, w_qkv, w_attn_out, w_in, w_out, attn_gain, mlp_gain, cotangent):
    seq_here, row_count, width_all = tokens.shape
    head_count = HEADS
    head_width = width_all // head_count
    scaling = head_width ** (-0.5)
    seq_len = row_count * lax.axis_size("ctx")
    block_len = math.gcd(seq_len, 1024)
    num_blocks = seq_len // block_len
    all_rows = seq_here * row_count
    per_head = (all_rows, head_count, head_width)

    def heads_first(rows):
        return jnp.transpose(
            rows.reshape(seq_here, row_count, head_count, head_width), (0, 2, 1, 3)
        )

    def heads_last(rows):
        return jnp.transpose(
            rows.reshape(seq_here, row_count, head_count, head_width), (0, 2, 3, 1)
        )

    def rows_from_first(stacked):
        return jnp.transpose(stacked, (0, 2, 1, 3)).reshape(per_head)

    def rows_from_last(stacked):
        return jnp.transpose(stacked, (0, 3, 1, 2)).reshape(per_head)

    full_qkv, full_attn, full_in, full_out, gain_one, gain_two = (
        lax.all_gather(w_qkv, "wsh", axis=0, tiled=True),
        lax.all_gather(w_attn_out, "wsh", axis=0, tiled=True),
        lax.all_gather(w_in, "wsh", axis=0, tiled=True),
        lax.all_gather(w_out, "wsh", axis=0, tiled=True),
        lax.all_gather(attn_gain, "wsh", axis=0, tiled=True),
        lax.all_gather(mlp_gain, "wsh", axis=0, tiled=True),
    )
    residual_in = tokens.reshape(all_rows, width_all).astype(jnp.float32)
    local_pos = lax.axis_index("ctx") * row_count + jnp.arange(row_count, dtype=jnp.int32)
    positions = jnp.tile(local_pos, seq_here)
    normed_f, norm_one_pull = jax.vjp(layer_norm, residual_in, gain_one.astype(jnp.float32))
    normed = normed_f.astype(jnp.bfloat16)
    joined_proj = jnp.dot(normed, full_qkv, preferred_element_type=jnp.float32)

    def rotate_pair(query_part, key_part):
        return (
            rotary(query_part.reshape(per_head), positions),
            rotary(key_part.reshape(per_head), positions),
        )

    (query_f, key_f), rotate_pull = jax.vjp(
        rotate_pair, joined_proj[:, :width_all], joined_proj[:, width_all : 2 * width_all]
    )
    query_rows_low = query_f.astype(jnp.bfloat16)
    queries = heads_first(query_rows_low)
    keys_own = heads_last(key_f.astype(jnp.bfloat16))
    values_own = heads_last(joined_proj[:, 2 * width_all :].astype(jnp.bfloat16))
    mask_own = key_mask.astype(jnp.bfloat16).reshape(seq_here, 1, 1, row_count)
    keys_all, values_all, mask_all = (
        lax.all_gather(keys_own, "ctx", axis=3, tiled=True),
        lax.all_gather(values_own, "ctx", axis=3, tiled=True),
        lax.all_gather(mask_own, "ctx", axis=3, tiled=True),
    )

    def remote_block(index):
        start = index * block_len
        return (
            lax.dynamic_slice_in_dim(keys_all, start, block_len, 3),
            lax.dynamic_slice_in_dim(values_all, start, block_len, 3),
            lax.dynamic_slice_in_dim(mask_all, start, block_len, 3),
        )

    def forward_step(carried, index):
        running_top, running_total, running_sum = carried
        key_block, value_block, mask_block = remote_block(index)
        raw_scores = (
            jnp.einsum("bhqd,bhdk->bhqk", queries, key_block, preferred_element_type=jnp.float32)
            * scaling
        )
        scores = jnp.where(mask_block > 0.5, raw_scores, MASKED)
        new_top = jnp.maximum(running_top, jnp.max(scores, axis=-1))
        fade_factor = jnp.exp(running_top - new_top)
        weights = jnp.exp(scores - new_top[..., None])
        running_total = running_total * fade_factor + jnp.sum(weights, axis=-1)
        running_sum = running_sum * fade_factor[..., None] + jnp.einsum(
            "bhqk,bhdk->bhqd",
            weights.astype(jnp.bfloat16),
            value_block,
            preferred_element_type=jnp.float32,
        )
        return ((new_top, running_total, running_sum), None)

    stat_shape = (seq_here, head_count, row_count)
    block_ids = jnp.arange(num_blocks, dtype=jnp.int32)
    start_state = (
        jnp.full(stat_shape, MASKED, jnp.float32),
        jnp.zeros(stat_shape, jnp.float32),
        jnp.zeros(stat_shape + (head_width,), jnp.float32),
    )
    (final_top, final_total, final_sum), unused_out = lax.scan(forward_step, start_state, block_ids)
    log_total = final_top + jnp.log(final_total)
    attended_heads = final_sum / final_total[..., None]
    attended = rows_from_first(attended_heads).reshape(all_rows, width_all).astype(jnp.bfloat16)
    hidden = residual_in + jnp.dot(attended, full_attn, preferred_element_type=jnp.float32)
    normed_two_f, norm_two_pull = jax.vjp(layer_norm, hidden, gain_two.astype(jnp.float32))
    normed_two = normed_two_f.astype(jnp.bfloat16)
    projected = jnp.dot(normed_two, full_in, preferred_element_type=jnp.float32)
    gated_f, glu_pull = jax.vjp(geglu, projected)
    gated = gated_f.astype(jnp.bfloat16)
    result = hidden + jnp.dot(gated, full_out, preferred_element_type=jnp.float32)
    outcome = result.astype(jnp.bfloat16).reshape(seq_here, row_count, width_all)
    grad_out = cotangent.reshape(all_rows, width_all)
    grad_w_out = jnp.dot(gated.T, grad_out, preferred_element_type=jnp.float32)
    grad_gated = jnp.dot(grad_out, full_out.T, preferred_element_type=jnp.float32)
    (grad_proj,) = glu_pull(grad_gated)
    grad_proj_low = grad_proj.astype(jnp.bfloat16)
    grad_w_in = jnp.dot(normed_two.T, grad_proj_low, preferred_element_type=jnp.float32)
    grad_norm_two = jnp.dot(grad_proj_low, full_in.T, preferred_element_type=jnp.float32)
    grad_hidden_ln, grad_gain_two = norm_two_pull(grad_norm_two)
    grad_hidden = grad_out.astype(jnp.float32) + grad_hidden_ln
    grad_branch = grad_hidden.astype(jnp.bfloat16)
    grad_w_attn = jnp.dot(attended.T, grad_branch, preferred_element_type=jnp.float32)
    grad_att_rows = (
        jnp.dot(grad_branch, full_attn.T, preferred_element_type=jnp.float32)
        .astype(jnp.bfloat16)
        .reshape(per_head)
    )
    grad_attended = heads_first(grad_att_rows)
    delta_heads = jnp.sum(grad_attended.astype(jnp.float32) * attended_heads, axis=-1)

    def remote_terms(index):
        key_block, value_block, mask_block = remote_block(index)
        raw_scores = (
            jnp.einsum("bhqd,bhdk->bhqk", queries, key_block, preferred_element_type=jnp.float32)
            * scaling
        )
        scores = jnp.where(mask_block > 0.5, raw_scores, MASKED)
        probability = jnp.exp(scores - log_total[..., None])
        grad_probs = jnp.einsum(
            "bhqd,bhdk->bhqk", grad_attended, value_block, preferred_element_type=jnp.float32
        )
        grad_scores = (probability * (grad_probs - delta_heads[..., None])).astype(jnp.bfloat16)
        grad_query_part = (
            jnp.einsum(
                "bhqk,bhdk->bhqd", grad_scores, key_block, preferred_element_type=jnp.float32
            )
            * scaling
        )
        return (probability, grad_scores, grad_query_part)

    whole_zeros = jnp.zeros((seq_here, head_count, head_width, seq_len), jnp.float32)

    def key_step(carried, index):
        grad_query_acc, key_terms, value_terms = carried
        probability, grad_scores, grad_query_part = remote_terms(index)
        grad_value_block = jnp.einsum(
            "bhqk,bhqd->bhdk",
            probability.astype(jnp.bfloat16),
            grad_attended,
            preferred_element_type=jnp.float32,
        )
        grad_key_block = (
            jnp.einsum("bhqk,bhqd->bhdk", grad_scores, queries, preferred_element_type=jnp.float32)
            * scaling
        )
        start = index * block_len
        key_terms = lax.dynamic_update_slice_in_dim(key_terms, grad_key_block, start, 3)
        value_terms = lax.dynamic_update_slice_in_dim(value_terms, grad_value_block, start, 3)
        return ((grad_query_acc + grad_query_part, key_terms, value_terms), None)

    (grad_query_heads, key_terms, value_terms), unused_steps = lax.scan(
        key_step,
        (jnp.zeros(stat_shape + (head_width,), jnp.float32), whole_zeros, whole_zeros),
        block_ids,
    )
    grad_key_heads, grad_value_heads = (
        lax.psum_scatter(key_terms, "ctx", scatter_dimension=3, tiled=True),
        lax.psum_scatter(value_terms, "ctx", scatter_dimension=3, tiled=True),
    )
    grad_query = rows_from_first(grad_query_heads)
    grad_key = rows_from_last(grad_key_heads)
    grad_value = rows_from_last(grad_value_heads)
    grad_query_pre, grad_key_pre = rotate_pull((grad_query, grad_key))
    grad_joined = jnp.concatenate(
        [grad_query_pre, grad_key_pre, grad_value.reshape(all_rows, width_all)], axis=1
    ).astype(jnp.bfloat16)
    grad_w_qkv = jnp.dot(normed.T, grad_joined, preferred_element_type=jnp.float32)
    grad_normed = jnp.dot(grad_joined, full_qkv.T, preferred_element_type=jnp.float32)
    grad_in_ln, grad_gain_one = norm_one_pull(grad_normed)
    grad_tokens = (
        (grad_hidden + grad_in_ln).astype(jnp.bfloat16).reshape(seq_here, row_count, width_all)
    )
    every_part = (
        lax.psum_scatter(
            grad_w_qkv.astype(jnp.bfloat16), "wsh", scatter_dimension=0, tiled=True
        ).astype(jnp.float32),
        lax.psum_scatter(
            grad_w_attn.astype(jnp.bfloat16), "wsh", scatter_dimension=0, tiled=True
        ).astype(jnp.float32),
        lax.psum_scatter(
            grad_w_in.astype(jnp.bfloat16), "wsh", scatter_dimension=0, tiled=True
        ).astype(jnp.float32),
        lax.psum_scatter(
            grad_w_out.astype(jnp.bfloat16), "wsh", scatter_dimension=0, tiled=True
        ).astype(jnp.float32),
        lax.psum_scatter(
            grad_gain_one.astype(jnp.bfloat16), "wsh", scatter_dimension=0, tiled=True
        ).astype(jnp.float32),
        lax.psum_scatter(
            grad_gain_two.astype(jnp.bfloat16), "wsh", scatter_dimension=0, tiled=True
        ).astype(jnp.float32),
    )
    sum_qkv, sum_attn, sum_in, sum_out, sum_gain_one, sum_gain_two = lax.psum(
        (every_part[0], every_part[1], every_part[2], every_part[3], every_part[4], every_part[5]),
        "ctx",
    )
    return (outcome, grad_tokens, sum_gain_one, sum_gain_two, sum_qkv, sum_attn, sum_in, sum_out)


NT = (((1,), (1,)), ((), ()))
NN = (((1,), (0,)), ((), ()))
TN = (((0,), (0,)), ((), ()))


def mm(left, right, dims=NN):
    return lax.dot_general(left, right, dims, preferred_element_type=jnp.float32)


def attend_kernel(q_ref, k_ref, v_ref, mask_ref, o_ref, p_ref):
    width = q_ref.shape[1]
    scores = mm(k_ref[0], q_ref[0], TN) * width ** (-0.5)
    scores = jnp.where(mask_ref[...] > 0.5, scores, MASKED)
    top = jnp.max(scores, axis=0, keepdims=True)
    weights = jnp.exp(scores - top)
    prob = weights * (1.0 / jnp.sum(weights, axis=0, keepdims=True))
    p_ref[0] = prob
    o_ref[0] = mm(v_ref[0], prob.astype(jnp.bfloat16))


def attend(queries, keys, values, mask_col):
    pairs, width, length = queries.shape
    rows = math.gcd(length, 256)
    one = lambda: pl.BlockSpec((1, width, length), lambda i, j: (i, 0, 0))
    part = lambda: pl.BlockSpec((1, width, rows), lambda i, j: (i, 0, j))
    return pl.pallas_call(
        attend_kernel,
        grid=(pairs, length // rows),
        in_specs=[part(), one(), one(), pl.BlockSpec((length, 1), lambda i, j: (0, 0))],
        out_specs=[part(), pl.BlockSpec((1, length, rows), lambda i, j: (i, 0, j))],
        out_shape=[
            jax.ShapeDtypeStruct((pairs, width, length), jnp.float32),
            jax.ShapeDtypeStruct((pairs, length, length), jnp.float32),
        ],
        compiler_params=pltpu.CompilerParams(vmem_limit_bytes=40 * 2**20),
        cost_estimate=pl.CostEstimate(
            flops=4 * pairs * width * length**2,
            bytes_accessed=4 * pairs * length**2,
            transcendentals=pairs * length**2,
        ),
    )(queries, keys, values, mask_col)


def attend_back_kernel(q_ref, k_ref, v_ref, do_ref, o_ref, p_ref, dq_ref, dk_ref, dv_ref):
    step = pl.program_id(1)
    scaling = q_ref.shape[1] ** (-0.5)
    grad_out = do_ref[0]
    delta = jnp.sum(grad_out.astype(jnp.float32) * o_ref[0], axis=0, keepdims=True)
    prob = p_ref[0]
    grad_prob = mm(v_ref[0], grad_out, TN)
    grad_scores = (prob * (grad_prob - delta)).astype(jnp.bfloat16)
    dq_ref[0] = mm(k_ref[0], grad_scores) * scaling

    @pl.when(step == 0)
    def _():
        dk_ref[...] = jnp.zeros_like(dk_ref)
        dv_ref[...] = jnp.zeros_like(dv_ref)

    dk_ref[0] += mm(q_ref[0], grad_scores, NT) * scaling
    dv_ref[0] += mm(grad_out, prob.astype(jnp.bfloat16), NT)


def attend_back(queries, keys, values, grad_out, mixed, prob):
    pairs, width, length = queries.shape
    rows = math.gcd(length, 256)
    one = lambda: pl.BlockSpec((1, width, length), lambda i, j: (i, 0, 0))
    part = lambda: pl.BlockSpec((1, width, rows), lambda i, j: (i, 0, j))
    shape = jax.ShapeDtypeStruct((pairs, width, length), jnp.float32)
    return pl.pallas_call(
        attend_back_kernel,
        grid=(pairs, length // rows),
        in_specs=[
            part(),
            one(),
            one(),
            part(),
            part(),
            pl.BlockSpec((1, length, rows), lambda i, j: (i, 0, j)),
        ],
        out_specs=[part(), one(), one()],
        out_shape=[shape, shape, shape],
        compiler_params=pltpu.CompilerParams(vmem_limit_bytes=40 * 2**20),
        cost_estimate=pl.CostEstimate(
            flops=8 * pairs * width * length**2,
            bytes_accessed=4 * pairs * length**2,
            transcendentals=0,
        ),
    )(queries, keys, values, grad_out, mixed, prob)


MESH = pl.DeviceIdType.MESH
CTX = 8
TILE = 16


class Place:
    def __init__(self):
        self.c, self.z = lax.axis_index("ctx"), lax.axis_index("wsh")
        self.core = lax.rem(self.c, 2)
        self.x = lax.rem(self.c // 2, 2)
        self.y = self.c // 4

    def flip(self, core=0, x=0, y=0):
        core = 1 - self.core if core else self.core
        x = 1 - self.x if x else self.x
        y = 1 - self.y if y else self.y
        return core, x, y

    def device(self, **axes):
        core, x, y = self.flip(**axes)
        return (y * 4 + x * 2 + core, self.z)

    def chip(self, **axes):
        core, x, y = self.flip(**axes)
        return y * 2 + x

    def piece(self, **axes):
        core, x, y = self.flip(**axes)
        return core * 4 + y * 2 + x


def greet(me, depth):
    barrier = pltpu.get_barrier_semaphore()
    for axes in ({"core": 1}, {"x": 1}, {"y": 1}):
        pl.semaphore_signal(barrier, inc=1, device_id=me.device(**axes), device_id_type=MESH)

    @pl.when(me.z > 0)
    def _():
        pl.semaphore_signal(barrier, inc=1, device_id=(me.c, me.z - 1), device_id_type=MESH)

    @pl.when(me.z < depth - 1)
    def _():
        pl.semaphore_signal(barrier, inc=1, device_id=(me.c, me.z + 1), device_id_type=MESH)

    line_peers = jnp.where(me.z > 0, 1, 0) + jnp.where(me.z < depth - 1, 1, 0)
    pl.semaphore_wait(barrier, 3 + line_peers)


def remote(src, dst, send, recv, device):
    return pltpu.make_async_remote_copy(
        src_ref=src, dst_ref=dst, send_sem=send, recv_sem=recv, device_id=device, device_id_type=MESH
    )


def rows_at(start, count):
    return pl.ds(pl.multiple_of(start, TILE), count)


def cut(size):
    first = (size // TILE + 1) // 2 * TILE
    return first, size - first


SPREAD = 9
X, Y, XY = {"x": 1}, {"y": 1}, {"x": 1, "y": 1}
CORE = {"core": 1}


def spread(me, size, own, buf, send, recv):
    first, second = cut(size)
    whole, one, two = (0, size), (0, first), (first, second)
    moves = (
        ({}, whole, X),
        ({}, whole, Y),
        ({}, whole, CORE),
        (X, one, Y),
        (X, whole, CORE),
        (Y, two, X),
        (Y, whole, CORE),
        (XY, one, CORE),
        (XY, two, CORE),
    )

    def region(axes, part):
        return buf(me.piece(**axes) * size + part[0], part[1])

    def sent(i):
        axes, part, to = moves[i]
        here = own if not axes else region(axes, part)
        return remote(here, region(axes, part), send(i), recv(i), me.device(**to))

    def arrived(i):
        axes, part, to = moves[i]
        source = {key: 1 for key in ("core", "x", "y") if (key in axes) != (key in to)}
        there = region(source, part)
        remote(there, there, send(i), recv(i), me.device(**to)).wait_recv()

    def begin():
        for i in (0, 1, 2):
            sent(i).start()

    def middle():
        arrived(0)
        sent(3).start()
        sent(4).start()
        arrived(1)
        sent(5).start()
        sent(6).start()

    def late():
        arrived(3)
        sent(7).start()
        arrived(5)
        sent(8).start()

    def finish():
        for i in (2, 4, 6, 7, 8):
            arrived(i)
        for i in range(SPREAD):
            sent(i).wait_send()

    return begin, middle, late, finish


def layout(arrays, lead, width):
    plan, start = [], 0
    for n, array in enumerate(arrays):
        rows = array.shape[0] // lead
        for i in range(array.shape[1] // width):
            plan.append((n, i * width, rows, start))
            start += rows
    return plan, start


def gather_kernel(count, *refs):
    parts, out = refs[:count], refs[count]
    line_send, line_recv, send, recv, local = refs[count + 1 :]
    depth, total, width = out.shape
    size = total // CTX
    me = Place()
    plan, used = layout(parts, 1, width)
    keeps = [
        pltpu.make_async_copy(
            parts[n].at[:, pl.ds(column, width)], out.at[me.z, pl.ds(start, rows)], local.at[m]
        )
        for m, (n, column, rows, start) in enumerate(plan)
    ]
    for keep in keeps:
        keep.start()
    greet(me, depth)
    for keep in keeps:
        keep.wait()
    mine = rows_at(me.piece() * size, size)

    def along(way, t):
        origin, to = (me.z - t, me.z + 1) if way == 0 else (me.z + t, me.z - 1)
        origin, to = jnp.clip(origin, 0, depth - 1), jnp.clip(to, 0, depth - 1)
        here = out.at[origin, mine]
        pair = (line_send.at[way, t], line_recv.at[way, t])
        return remote(here, out.at[origin, mine], *pair, (me.c, to))

    def goes(way, t):
        if way == 0:
            return (me.z >= t) & (me.z + 1 < depth)
        return (me.z + t < depth) & (me.z >= 1)

    def comes(way, t):
        return me.z >= t if way == 0 else me.z + t < depth

    def steps(way, t):
        origin = jnp.clip(me.z - t if way == 0 else me.z + t, 0, depth - 1)
        slot = way * (depth - 1) + t - 1
        return spread(
            me,
            size,
            out.at[origin, mine],
            lambda start, count: out.at[origin, rows_at(start, count)],
            lambda i: send.at[slot, i],
            lambda i: recv.at[slot, i],
        )

    for way in (0, 1):

        @pl.when(goes(way, 0))
        def _():
            along(way, 0).start()

    for t in range(1, depth + 2):
        for way in (0, 1):
            if t < depth:

                @pl.when(comes(way, t))
                def _():
                    origin = jnp.clip(me.z - t if way == 0 else me.z + t, 0, depth - 1)
                    there = out.at[origin, mine]
                    pair = (line_send.at[way, t - 1], line_recv.at[way, t - 1])
                    remote(there, there, *pair, me.device(**X)).wait_recv()
                    if t < depth - 1:

                        @pl.when(goes(way, t))
                        def _():
                            along(way, t).start()

                    steps(way, t)[0]()

        for way in (0, 1):
            if 1 <= t - 1 < depth:

                @pl.when(comes(way, t - 1))
                def _():
                    steps(way, t - 1)[1]()

        for way in (0, 1):
            if 1 <= t - 2 < depth:

                @pl.when(comes(way, t - 2))
                def _():
                    steps(way, t - 2)[2]()

    for way in (0, 1):
        for t in range(1, depth):

            @pl.when(comes(way, t))
            def _():
                steps(way, t)[3]()

        for t in range(depth - 1):

            @pl.when(goes(way, t))
            def _():
                along(way, t).wait_send()


def gather_packed(parts, width):
    depth = lax.axis_size("wsh")
    dma = pltpu.SemaphoreType.DMA
    plan, used = layout(parts, 1, width)
    return pl.pallas_call(
        functools.partial(gather_kernel, len(parts)),
        out_shape=jax.ShapeDtypeStruct((depth, used, width), parts[0].dtype),
        in_specs=[pl.BlockSpec(memory_space=pl.ANY)] * len(parts),
        out_specs=pl.BlockSpec(memory_space=pl.ANY),
        scratch_shapes=[
            dma((2, depth - 1)),
            dma((2, depth - 1)),
            dma((2 * (depth - 1), SPREAD)),
            dma((2 * (depth - 1), SPREAD)),
            dma((len(plan),)),
        ],
        compiler_params=pltpu.CompilerParams(collective_id=1, has_side_effects=True),
    )(*parts)


def add_rows(total, start, terms, count):
    def body(i, carry):
        at = rows_at(start + i * TILE, TILE)
        value = total[at, :].astype(jnp.float32)
        for ref, base in terms:
            value = value + ref[rows_at(base + i * TILE, TILE), :].astype(jnp.float32)
        total[at, :] = value.astype(total.dtype)
        return carry

    lax.fori_loop(0, count // TILE, body, 0)


def reduce_kernel(count, *refs):
    parts, out = refs[:count], refs[count]
    total, pair, near_x, near_y, last, line = refs[count + 1 : count + 7]
    local, core_send, core_recv, near_send, near_recv = refs[count + 7 : count + 12]
    line_send, line_recv, send, recv, keep_sem = refs[count + 12 :]
    depth, size, width = last.shape
    half = 4 * size
    first, second = cut(size)
    me = Place()
    k, kx, ky, kd = me.chip(), me.chip(**X), me.chip(**Y), me.chip(**XY)
    to_x, to_y, to_core = me.device(**X), me.device(**Y), me.device(**CORE)

    def cores(zz):
        return remote(
            total.at[zz, rows_at((1 - me.core) * half, half)],
            pair.at[zz],
            core_send.at[zz],
            core_recv.at[zz],
            to_core,
        )

    plan, used = layout(parts, depth, width)
    base = me.core * half

    def own(zz):
        return [
            pltpu.make_async_copy(
                parts[n].at[pl.ds(zz * rows, rows), pl.ds(column, width)],
                total.at[zz, pl.ds(start, rows)],
                local.at[zz, m],
            )
            for m, (n, column, rows, start) in enumerate(plan)
        ]

    def near(zz, i):
        sems = (near_send.at[zz, i], near_recv.at[zz, i])
        part = lambda chip, offset, count: total.at[zz, rows_at(base + chip * size + offset, count)]
        if i == 0:
            return remote(part(kd, 0, first), near_x.at[zz, 1], *sems, to_x)
        if i == 1:
            return remote(part(kd, first, second), near_y.at[zz, 1], *sems, to_y)
        if i == 2:
            return remote(part(kx, 0, first), near_x.at[zz, 0], *sems, to_x)
        if i == 3:
            return remote(part(ky, first, second), near_y.at[zz, 0], *sems, to_y)
        if i == 4:
            return remote(part(ky, 0, first), last.at[zz, pl.ds(0, first)], *sems, to_y)
        return remote(part(kx, first, second), last.at[zz, pl.ds(first, second)], *sems, to_x)

    for zz in range(depth):
        for copy in own(zz):
            copy.start()
    greet(me, depth)
    for zz in range(depth):
        for copy in own(zz):
            copy.wait()
        cores(zz).start()
    for t in range(depth + 2):
        if t < depth:
            cores(t).wait_recv()
            add_rows(total.at[t], base, [(pair.at[t], 0)], half)
            for i in range(4):
                near(t, i).start()
        if 0 <= t - 1 < depth:
            zz = t - 1
            near(zz, 0).wait_recv()
            add_rows(total.at[zz], base + ky * size, [(near_x.at[zz, 1], 0)], first)
            near(zz, 4).start()
            near(zz, 1).wait_recv()
            add_rows(total.at[zz], base + kx * size + first, [(near_y.at[zz, 1], 0)], second)
            near(zz, 5).start()
        if 0 <= t - 2 < depth:
            zz = t - 2
            near(zz, 2).wait_recv()
            near(zz, 4).wait_recv()
            add_rows(total.at[zz], base + k * size, [(near_x.at[zz, 0], 0), (last.at[zz], 0)], first)
            near(zz, 3).wait_recv()
            near(zz, 5).wait_recv()
            terms = [(near_y.at[zz, 0], 0), (last.at[zz], first)]
            add_rows(total.at[zz], base + k * size + first, terms, second)

    mine = rows_at(base + k * size, size)

    def along(way, zz):
        to = jnp.clip(me.z - 1 if way == 0 else me.z + 1, 0, depth - 1)
        sems = (line_send.at[way, zz], line_recv.at[way, zz])
        return remote(total.at[zz, mine], line.at[way, zz], *sems, (me.c, to))

    def goes(way, zz):
        return zz < me.z if way == 0 else zz > me.z

    def fed(way):
        return me.z + 1 < depth if way == 0 else me.z >= 1

    def take(way, zz):
        @pl.when(fed(way))
        def _():
            along(way, zz).wait_recv()
            add_rows(total.at[zz], base + k * size, [(line.at[way, zz], 0)], size)

    for j in range(depth):
        for way, zz in ((0, j), (1, depth - 1 - j)):

            @pl.when(goes(way, zz))
            def _():
                take(way, zz)
                along(way, zz).start()

    take(0, me.z)
    take(1, me.z)
    done = total.at[me.z, mine]
    begin, middle, late, finish = spread(
        me,
        size,
        done,
        lambda start, count: out.at[rows_at(start, count)],
        lambda i: send.at[i],
        lambda i: recv.at[i],
    )
    begin()
    keep = pltpu.make_async_copy(done, out.at[rows_at(me.piece() * size, size)], keep_sem)
    keep.start()
    middle()
    late()
    finish()
    keep.wait()
    for zz in range(depth):
        cores(zz).wait_send()
        for i in range(6):
            near(zz, i).wait_send()
        for way in (0, 1):

            @pl.when(goes(way, zz))
            def _():
                along(way, zz).wait_send()


def reduce_packed(parts, width):
    depth = lax.axis_size("wsh")
    plan, rows = layout(parts, depth, width)
    size = rows // CTX
    first, second = cut(size)
    dma = pltpu.SemaphoreType.DMA
    low = parts[0].dtype
    return pl.pallas_call(
        functools.partial(reduce_kernel, len(parts)),
        out_shape=jax.ShapeDtypeStruct((rows, width), low),
        in_specs=[pl.BlockSpec(memory_space=pl.ANY)] * len(parts),
        out_specs=pl.BlockSpec(memory_space=pl.ANY),
        scratch_shapes=[
            pltpu.VMEM((depth, rows, width), low),
            pltpu.VMEM((depth, 4 * size, width), low),
            pltpu.VMEM((depth, 2, first, width), low),
            pltpu.VMEM((depth, 2, second, width), low),
            pltpu.VMEM((depth, size, width), low),
            pltpu.VMEM((2, depth, size, width), low),
            dma((depth, len(plan))),
            dma((depth,)),
            dma((depth,)),
            dma((depth, 6)),
            dma((depth, 6)),
            dma((2, depth)),
            dma((2, depth)),
            dma((SPREAD,)),
            dma((SPREAD,)),
            dma,
        ],
        compiler_params=pltpu.CompilerParams(
            collective_id=2, has_side_effects=True, vmem_limit_bytes=48 * 2**20
        ),
    )(*parts)


def spare_rows(used):
    step = CTX * TILE
    return (used + 2 + step - 1) // step * step - used


def by_heads(tokens, key_mask, w_qkv, w_attn_out, w_in, w_out, attn_gain, mlp_gain, cotangent):
    seqs, rows, width = tokens.shape
    peers = lax.axis_size("ctx")
    head_width = width // HEADS
    half = head_width // 2
    pairs = seqs * HEADS // peers
    splits = peers // seqs
    feats = pairs * head_width
    length = rows * peers
    tokens_here = seqs * rows
    low = jnp.bfloat16

    depth = lax.axis_size("wsh")
    share, shape_out = w_qkv.shape[0], w_out.shape
    blocks = w_qkv.shape[1] // width
    blocks_in = w_in.shape[1] // width

    used = (blocks + 1 + blocks_in) * share + shape_out[0]
    spare = spare_rows(used)
    gain_rows = jnp.pad(
        jnp.stack([attn_gain, mlp_gain]), ((0, spare - 2), (0, width - share))
    )
    packed = gather_packed([w_qkv, w_attn_out, w_in, w_out, gain_rows], width)

    def unfold(start, rows_each, count):
        return jnp.concatenate(
            [
                packed[:, start + i * rows_each : start + (i + 1) * rows_each].reshape(-1, width)
                for i in range(count)
            ],
            axis=1,
        )

    at_attn = blocks * share
    at_in = at_attn + share
    at_out = at_in + blocks_in * share
    at_gain = at_out + shape_out[0]
    full_qkv = unfold(0, share, blocks)
    full_attn = unfold(at_attn, share, 1)
    full_in = unfold(at_in, share, blocks_in)
    full_out = unfold(at_out, shape_out[0], 1)
    gain_one = packed[:, at_gain, :share].reshape(-1)
    gain_two = packed[:, at_gain + 1, :share].reshape(-1)

    def to_heads(parts):
        count = parts.shape[0]
        sent = jnp.transpose(
            parts.reshape(count, splits, feats, seqs, rows), (3, 1, 0, 2, 4)
        ).reshape(peers, count * feats, rows)
        return sent

    def swap(sent):
        return lax.all_to_all(sent, "ctx", split_axis=0, concat_axis=0, tiled=True)

    def to_rows(parts):
        count = parts.shape[0]
        sent = jnp.transpose(
            parts.astype(low).reshape(count * feats, peers, rows), (1, 0, 2)
        )
        got = swap(sent).reshape(seqs, splits, count, feats, rows)
        return jnp.transpose(got, (2, 1, 3, 0, 4)).reshape(count, width, tokens_here)

    residual_in = tokens.reshape(tokens_here, width).astype(jnp.float32)
    normed_f, norm_one_pull = jax.vjp(layer_norm, residual_in, gain_one.astype(jnp.float32))
    normed = normed_f.astype(low)
    joined = mm(full_qkv, normed, (((0,), (1,)), ((), ())))

    local_pos = lax.axis_index("ctx") * rows + jnp.arange(rows, dtype=jnp.int32)
    inverse = jnp.exp(
        jnp.arange(half, dtype=jnp.float32) * (-2.0 * math.log(THETA) / head_width)
    )
    angles = inverse[:, None] * jnp.tile(local_pos, seqs).astype(jnp.float32)[None, :]
    cosine, sine = jnp.cos(angles), jnp.sin(angles)

    def turn(values, way):
        pair = values.reshape(HEADS, 2, half, tokens_here)
        first, second = pair[:, 0], pair[:, 1]
        return jnp.stack(
            [first * cosine - way * (second * sine), second * cosine + way * (first * sine)], axis=1
        ).reshape(width, tokens_here)

    trio = jnp.stack(
        [turn(joined[:width], 1.0), turn(joined[width : 2 * width], 1.0), joined[2 * width :]]
    ).astype(low)
    mask_rows = jnp.broadcast_to(
        key_mask.astype(low)[:, None, None, :], (seqs, splits, 16, rows)
    ).reshape(peers, 16, rows)
    got = swap(jnp.concatenate([to_heads(trio), mask_rows], axis=1))
    got = jnp.transpose(got, (1, 0, 2)).reshape(3 * feats + 16, length)
    queries, keys, values = (
        got[i * feats : (i + 1) * feats].reshape(pairs, head_width, length) for i in range(3)
    )
    mask_col = got[3 * feats].astype(jnp.float32)[:, None]
    mixed, prob = attend(queries, keys, values, mask_col)
    attended = jnp.transpose(to_rows(mixed.reshape(1, feats, length))[0])

    hidden = residual_in + mm(attended, full_attn)
    normed_two_f, norm_two_pull = jax.vjp(layer_norm, hidden, gain_two.astype(jnp.float32))
    normed_two = normed_two_f.astype(low)
    projected = mm(normed_two, full_in)
    gated_f, glu_pull = jax.vjp(geglu, projected)
    gated = gated_f.astype(low)
    outcome = (hidden + mm(gated, full_out)).astype(low).reshape(seqs, rows, width)
    grad_out = cotangent.reshape(tokens_here, width)
    term_out = mm(gated, grad_out, TN).astype(low)
    (grad_proj,) = glu_pull(mm(grad_out, full_out, NT))
    grad_proj = grad_proj.astype(low)
    term_in = mm(normed_two, grad_proj, TN).astype(low)
    grad_hidden_ln, grad_gain_two = norm_two_pull(mm(grad_proj, full_in, NT))
    grad_hidden = grad_out.astype(jnp.float32) + grad_hidden_ln
    grad_branch = grad_hidden.astype(low)
    term_attn = mm(attended, grad_branch, TN).astype(low)
    grad_att = mm(full_attn, grad_branch, NT).astype(low)
    got_do = swap(to_heads(grad_att[None]))
    got_do = jnp.transpose(got_do, (1, 0, 2)).reshape(pairs, head_width, length)
    grads = attend_back(queries, keys, values, got_do, mixed, prob)
    back = to_rows(jnp.stack([g.reshape(feats, length) for g in grads])).astype(jnp.float32)
    grad_joined = jnp.concatenate([turn(back[0], -1.0), turn(back[1], -1.0), back[2]]).astype(low)
    term_qkv = mm(normed, grad_joined, (((0,), (1,)), ((), ()))).astype(low)
    grad_normed = mm(grad_joined, full_qkv, (((0,), (1,)), ((), ())))
    grad_in_ln, grad_gain_one = norm_one_pull(grad_normed)
    grad_tokens = (grad_hidden + grad_in_ln).astype(low).reshape(seqs, rows, width)
    gain_terms = jnp.stack([grad_gain_one, grad_gain_two]).astype(low)
    gain_terms = jnp.transpose(gain_terms.reshape(2, depth, share), (1, 0, 2))

    gain_terms = jnp.pad(gain_terms, ((0, 0), (0, spare - 2), (0, width - share)))
    terms = [term_qkv, term_attn, term_in, term_out, gain_terms.reshape(-1, width)]
    sums = reduce_packed(terms, width).astype(jnp.float32)

    def side(start, count):
        return jnp.concatenate(
            [sums[start + i * share : start + (i + 1) * share] for i in range(count)], axis=1
        )

    return (
        outcome,
        grad_tokens,
        sums[at_gain, :share],
        sums[at_gain + 1, :share],
        side(0, blocks),
        side(at_attn, 1),
        side(at_in, blocks_in),
        sums[at_out : at_out + shape_out[0]],
    )


def shards(*arrays):
    seqs = arrays[0].shape[0]
    peers = lax.axis_size("ctx")
    even = (seqs * HEADS) % peers == 0 and peers % seqs == 0 and peers == CTX
    even = even and lax.axis_size("wsh") > 1 and arrays[4].shape[1] % arrays[0].shape[2] == 0
    return (by_heads if even else by_positions)(*arrays)


def solution(mesh):
    return jax.shard_map(
        shards,
        mesh=mesh,
        in_specs=(
            P("wsh", "ctx", None),
            P("wsh", "ctx"),
            P("wsh", None),
            P("wsh", None),
            P("wsh", None),
            P("wsh", None),
            P("wsh"),
            P("wsh"),
            P("wsh", "ctx", None),
        ),
        out_specs=(
            P("wsh", "ctx", None),
            P("wsh", "ctx", None),
            P("wsh"),
            P("wsh"),
            P("wsh", None),
            P("wsh", None),
            P("wsh", None),
            P("wsh", None),
        ),
        check_vma=False,
    )
```

```python
import functools
import math

import jax
import jax.numpy as jnp
from jax import lax
from jax.experimental import pallas as pl
from jax.experimental.pallas import tpu as pltpu
from jax.sharding import PartitionSpec as P

HEADS = 12


EPSILON = 1e-05
THETA = 160000.0
MASKED = -1e30


def layer_norm(values, gain):
    centred = values - jnp.mean(values, axis=-1, keepdims=True)
    spread = jnp.mean(centred * centred, axis=-1, keepdims=True)
    return centred * lax.rsqrt(spread + EPSILON) * gain


def rotary(heads_in, positions):
    half_dim = heads_in.shape[-1] // 2
    counter = jnp.arange(half_dim, dtype=jnp.float32)
    inverse = jnp.exp(counter * (-2.0 * math.log(THETA) / heads_in.shape[-1]))
    angles = positions.astype(jnp.float32)[:, None] * inverse[None, :]
    cosine = jnp.cos(angles)[:, None, :]
    sine_part = jnp.sin(angles)[:, None, :]
    first_half = heads_in[..., :half_dim]
    second = heads_in[..., half_dim:]
    return jnp.concatenate(
        [first_half * cosine - second * sine_part, second * cosine + first_half * sine_part],
        axis=-1,
    )


def geglu(projected):
    half_width = projected.shape[-1] // 2
    inner_part = projected[:, :half_width]
    gating = projected[:, half_width:]
    return 0.5 * inner_part * (1.0 + lax.erf(inner_part * 0.5**0.5)) * gating


def by_positions(tokens, key_mask, w_qkv, w_attn_out, w_in, w_out, attn_gain, mlp_gain, cotangent):
    seq_here, row_count, width_all = tokens.shape
    head_count = HEADS
    head_width = width_all // head_count
    scaling = head_width ** (-0.5)
    seq_len = row_count * lax.axis_size("ctx")
    block_len = math.gcd(seq_len, 1024)
    num_blocks = seq_len // block_len
    all_rows = seq_here * row_count
    per_head = (all_rows, head_count, head_width)

    def heads_first(rows):
        return jnp.transpose(
            rows.reshape(seq_here, row_count, head_count, head_width), (0, 2, 1, 3)
        )

    def heads_last(rows):
        return jnp.transpose(
            rows.reshape(seq_here, row_count, head_count, head_width), (0, 2, 3, 1)
        )

    def rows_from_first(stacked):
        return jnp.transpose(stacked, (0, 2, 1, 3)).reshape(per_head)

    def rows_from_last(stacked):
        return jnp.transpose(stacked, (0, 3, 1, 2)).reshape(per_head)

    full_qkv, full_attn, full_in, full_out, gain_one, gain_two = (
        lax.all_gather(w_qkv, "wsh", axis=0, tiled=True),
        lax.all_gather(w_attn_out, "wsh", axis=0, tiled=True),
        lax.all_gather(w_in, "wsh", axis=0, tiled=True),
        lax.all_gather(w_out, "wsh", axis=0, tiled=True),
        lax.all_gather(attn_gain, "wsh", axis=0, tiled=True),
        lax.all_gather(mlp_gain, "wsh", axis=0, tiled=True),
    )
    residual_in = tokens.reshape(all_rows, width_all).astype(jnp.float32)
    local_pos = lax.axis_index("ctx") * row_count + jnp.arange(row_count, dtype=jnp.int32)
    positions = jnp.tile(local_pos, seq_here)
    normed_f, norm_one_pull = jax.vjp(layer_norm, residual_in, gain_one.astype(jnp.float32))
    normed = normed_f.astype(jnp.bfloat16)
    joined_proj = jnp.dot(normed, full_qkv, preferred_element_type=jnp.float32)

    def rotate_pair(query_part, key_part):
        return (
            rotary(query_part.reshape(per_head), positions),
            rotary(key_part.reshape(per_head), positions),
        )

    (query_f, key_f), rotate_pull = jax.vjp(
        rotate_pair, joined_proj[:, :width_all], joined_proj[:, width_all : 2 * width_all]
    )
    query_rows_low = query_f.astype(jnp.bfloat16)
    queries = heads_first(query_rows_low)
    keys_own = heads_last(key_f.astype(jnp.bfloat16))
    values_own = heads_last(joined_proj[:, 2 * width_all :].astype(jnp.bfloat16))
    mask_own = key_mask.astype(jnp.bfloat16).reshape(seq_here, 1, 1, row_count)
    keys_all, values_all, mask_all = (
        lax.all_gather(keys_own, "ctx", axis=3, tiled=True),
        lax.all_gather(values_own, "ctx", axis=3, tiled=True),
        lax.all_gather(mask_own, "ctx", axis=3, tiled=True),
    )

    def remote_block(index):
        start = index * block_len
        return (
            lax.dynamic_slice_in_dim(keys_all, start, block_len, 3),
            lax.dynamic_slice_in_dim(values_all, start, block_len, 3),
            lax.dynamic_slice_in_dim(mask_all, start, block_len, 3),
        )

    def forward_step(carried, index):
        running_top, running_total, running_sum = carried
        key_block, value_block, mask_block = remote_block(index)
        raw_scores = (
            jnp.einsum("bhqd,bhdk->bhqk", queries, key_block, preferred_element_type=jnp.float32)
            * scaling
        )
        scores = jnp.where(mask_block > 0.5, raw_scores, MASKED)
        new_top = jnp.maximum(running_top, jnp.max(scores, axis=-1))
        fade_factor = jnp.exp(running_top - new_top)
        weights = jnp.exp(scores - new_top[..., None])
        running_total = running_total * fade_factor + jnp.sum(weights, axis=-1)
        running_sum = running_sum * fade_factor[..., None] + jnp.einsum(
            "bhqk,bhdk->bhqd",
            weights.astype(jnp.bfloat16),
            value_block,
            preferred_element_type=jnp.float32,
        )
        return ((new_top, running_total, running_sum), None)

    stat_shape = (seq_here, head_count, row_count)
    block_ids = jnp.arange(num_blocks, dtype=jnp.int32)
    start_state = (
        jnp.full(stat_shape, MASKED, jnp.float32),
        jnp.zeros(stat_shape, jnp.float32),
        jnp.zeros(stat_shape + (head_width,), jnp.float32),
    )
    (final_top, final_total, final_sum), unused_out = lax.scan(forward_step, start_state, block_ids)
    log_total = final_top + jnp.log(final_total)
    attended_heads = final_sum / final_total[..., None]
    attended = rows_from_first(attended_heads).reshape(all_rows, width_all).astype(jnp.bfloat16)
    hidden = residual_in + jnp.dot(attended, full_attn, preferred_element_type=jnp.float32)
    normed_two_f, norm_two_pull = jax.vjp(layer_norm, hidden, gain_two.astype(jnp.float32))
    normed_two = normed_two_f.astype(jnp.bfloat16)
    projected = jnp.dot(normed_two, full_in, preferred_element_type=jnp.float32)
    gated_f, glu_pull = jax.vjp(geglu, projected)
    gated = gated_f.astype(jnp.bfloat16)
    result = hidden + jnp.dot(gated, full_out, preferred_element_type=jnp.float32)
    outcome = result.astype(jnp.bfloat16).reshape(seq_here, row_count, width_all)
    grad_out = cotangent.reshape(all_rows, width_all)
    grad_w_out = jnp.dot(gated.T, grad_out, preferred_element_type=jnp.float32)
    grad_gated = jnp.dot(grad_out, full_out.T, preferred_element_type=jnp.float32)
    (grad_proj,) = glu_pull(grad_gated)
    grad_proj_low = grad_proj.astype(jnp.bfloat16)
    grad_w_in = jnp.dot(normed_two.T, grad_proj_low, preferred_element_type=jnp.float32)
    grad_norm_two = jnp.dot(grad_proj_low, full_in.T, preferred_element_type=jnp.float32)
    grad_hidden_ln, grad_gain_two = norm_two_pull(grad_norm_two)
    grad_hidden = grad_out.astype(jnp.float32) + grad_hidden_ln
    grad_branch = grad_hidden.astype(jnp.bfloat16)
    grad_w_attn = jnp.dot(attended.T, grad_branch, preferred_element_type=jnp.float32)
    grad_att_rows = (
        jnp.dot(grad_branch, full_attn.T, preferred_element_type=jnp.float32)
        .astype(jnp.bfloat16)
        .reshape(per_head)
    )
    grad_attended = heads_first(grad_att_rows)
    delta_heads = jnp.sum(grad_attended.astype(jnp.float32) * attended_heads, axis=-1)

    def remote_terms(index):
        key_block, value_block, mask_block = remote_block(index)
        raw_scores = (
            jnp.einsum("bhqd,bhdk->bhqk", queries, key_block, preferred_element_type=jnp.float32)
            * scaling
        )
        scores = jnp.where(mask_block > 0.5, raw_scores, MASKED)
        probability = jnp.exp(scores - log_total[..., None])
        grad_probs = jnp.einsum(
            "bhqd,bhdk->bhqk", grad_attended, value_block, preferred_element_type=jnp.float32
        )
        grad_scores = (probability * (grad_probs - delta_heads[..., None])).astype(jnp.bfloat16)
        grad_query_part = (
            jnp.einsum(
                "bhqk,bhdk->bhqd", grad_scores, key_block, preferred_element_type=jnp.float32
            )
            * scaling
        )
        return (probability, grad_scores, grad_query_part)

    whole_zeros = jnp.zeros((seq_here, head_count, head_width, seq_len), jnp.float32)

    def key_step(carried, index):
        grad_query_acc, key_terms, value_terms = carried
        probability, grad_scores, grad_query_part = remote_terms(index)
        grad_value_block = jnp.einsum(
            "bhqk,bhqd->bhdk",
            probability.astype(jnp.bfloat16),
            grad_attended,
            preferred_element_type=jnp.float32,
        )
        grad_key_block = (
            jnp.einsum("bhqk,bhqd->bhdk", grad_scores, queries, preferred_element_type=jnp.float32)
            * scaling
        )
        start = index * block_len
        key_terms = lax.dynamic_update_slice_in_dim(key_terms, grad_key_block, start, 3)
        value_terms = lax.dynamic_update_slice_in_dim(value_terms, grad_value_block, start, 3)
        return ((grad_query_acc + grad_query_part, key_terms, value_terms), None)

    (grad_query_heads, key_terms, value_terms), unused_steps = lax.scan(
        key_step,
        (jnp.zeros(stat_shape + (head_width,), jnp.float32), whole_zeros, whole_zeros),
        block_ids,
    )
    grad_key_heads, grad_value_heads = (
        lax.psum_scatter(key_terms, "ctx", scatter_dimension=3, tiled=True),
        lax.psum_scatter(value_terms, "ctx", scatter_dimension=3, tiled=True),
    )
    grad_query = rows_from_first(grad_query_heads)
    grad_key = rows_from_last(grad_key_heads)
    grad_value = rows_from_last(grad_value_heads)
    grad_query_pre, grad_key_pre = rotate_pull((grad_query, grad_key))
    grad_joined = jnp.concatenate(
        [grad_query_pre, grad_key_pre, grad_value.reshape(all_rows, width_all)], axis=1
    ).astype(jnp.bfloat16)
    grad_w_qkv = jnp.dot(normed.T, grad_joined, preferred_element_type=jnp.float32)
    grad_normed = jnp.dot(grad_joined, full_qkv.T, preferred_element_type=jnp.float32)
    grad_in_ln, grad_gain_one = norm_one_pull(grad_normed)
    grad_tokens = (
        (grad_hidden + grad_in_ln).astype(jnp.bfloat16).reshape(seq_here, row_count, width_all)
    )
    every_part = (
        lax.psum_scatter(
            grad_w_qkv.astype(jnp.bfloat16), "wsh", scatter_dimension=0, tiled=True
        ).astype(jnp.float32),
        lax.psum_scatter(
            grad_w_attn.astype(jnp.bfloat16), "wsh", scatter_dimension=0, tiled=True
        ).astype(jnp.float32),
        lax.psum_scatter(
            grad_w_in.astype(jnp.bfloat16), "wsh", scatter_dimension=0, tiled=True
        ).astype(jnp.float32),
        lax.psum_scatter(
            grad_w_out.astype(jnp.bfloat16), "wsh", scatter_dimension=0, tiled=True
        ).astype(jnp.float32),
        lax.psum_scatter(
            grad_gain_one.astype(jnp.bfloat16), "wsh", scatter_dimension=0, tiled=True
        ).astype(jnp.float32),
        lax.psum_scatter(
            grad_gain_two.astype(jnp.bfloat16), "wsh", scatter_dimension=0, tiled=True
        ).astype(jnp.float32),
    )
    sum_qkv, sum_attn, sum_in, sum_out, sum_gain_one, sum_gain_two = lax.psum(
        (every_part[0], every_part[1], every_part[2], every_part[3], every_part[4], every_part[5]),
        "ctx",
    )
    return (outcome, grad_tokens, sum_gain_one, sum_gain_two, sum_qkv, sum_attn, sum_in, sum_out)


NT = (((1,), (1,)), ((), ()))
NN = (((1,), (0,)), ((), ()))
TN = (((0,), (0,)), ((), ()))


def mm(left, right, dims=NN):
    return lax.dot_general(left, right, dims, preferred_element_type=jnp.float32)


def attend_kernel(q_ref, k_ref, v_ref, mask_ref, o_ref, p_ref):
    width = q_ref.shape[1]
    scores = mm(k_ref[0], q_ref[0], TN) * width ** (-0.5)
    scores = jnp.where(mask_ref[...] > 0.5, scores, MASKED)
    top = jnp.max(scores, axis=0, keepdims=True)
    weights = jnp.exp(scores - top)
    prob = weights * (1.0 / jnp.sum(weights, axis=0, keepdims=True))
    p_ref[0] = prob
    o_ref[0] = mm(v_ref[0], prob.astype(jnp.bfloat16))


def attend(queries, keys, values, mask_col):
    pairs, width, length = queries.shape
    rows = math.gcd(length, 256)
    one = lambda: pl.BlockSpec((1, width, length), lambda i, j: (i, 0, 0))
    part = lambda: pl.BlockSpec((1, width, rows), lambda i, j: (i, 0, j))
    return pl.pallas_call(
        attend_kernel,
        grid=(pairs, length // rows),
        in_specs=[part(), one(), one(), pl.BlockSpec((length, 1), lambda i, j: (0, 0))],
        out_specs=[part(), pl.BlockSpec((1, length, rows), lambda i, j: (i, 0, j))],
        out_shape=[
            jax.ShapeDtypeStruct((pairs, width, length), jnp.float32),
            jax.ShapeDtypeStruct((pairs, length, length), jnp.float32),
        ],
        compiler_params=pltpu.CompilerParams(vmem_limit_bytes=40 * 2**20),
        cost_estimate=pl.CostEstimate(
            flops=4 * pairs * width * length**2,
            bytes_accessed=4 * pairs * length**2,
            transcendentals=pairs * length**2,
        ),
    )(queries, keys, values, mask_col)


def attend_back_kernel(q_ref, k_ref, v_ref, do_ref, o_ref, p_ref, dq_ref, dk_ref, dv_ref):
    step = pl.program_id(1)
    scaling = q_ref.shape[1] ** (-0.5)
    grad_out = do_ref[0]
    delta = jnp.sum(grad_out.astype(jnp.float32) * o_ref[0], axis=0, keepdims=True)
    prob = p_ref[0]
    grad_prob = mm(v_ref[0], grad_out, TN)
    grad_scores = (prob * (grad_prob - delta)).astype(jnp.bfloat16)
    dq_ref[0] = mm(k_ref[0], grad_scores) * scaling

    @pl.when(step == 0)
    def _():
        dk_ref[...] = jnp.zeros_like(dk_ref)
        dv_ref[...] = jnp.zeros_like(dv_ref)

    dk_ref[0] += mm(q_ref[0], grad_scores, NT) * scaling
    dv_ref[0] += mm(grad_out, prob.astype(jnp.bfloat16), NT)


def attend_back(queries, keys, values, grad_out, mixed, prob):
    pairs, width, length = queries.shape
    rows = math.gcd(length, 256)
    one = lambda: pl.BlockSpec((1, width, length), lambda i, j: (i, 0, 0))
    part = lambda: pl.BlockSpec((1, width, rows), lambda i, j: (i, 0, j))
    shape = jax.ShapeDtypeStruct((pairs, width, length), jnp.float32)
    return pl.pallas_call(
        attend_back_kernel,
        grid=(pairs, length // rows),
        in_specs=[
            part(),
            one(),
            one(),
            part(),
            part(),
            pl.BlockSpec((1, length, rows), lambda i, j: (i, 0, j)),
        ],
        out_specs=[part(), one(), one()],
        out_shape=[shape, shape, shape],
        compiler_params=pltpu.CompilerParams(vmem_limit_bytes=40 * 2**20),
        cost_estimate=pl.CostEstimate(
            flops=8 * pairs * width * length**2,
            bytes_accessed=4 * pairs * length**2,
            transcendentals=0,
        ),
    )(queries, keys, values, grad_out, mixed, prob)


MESH = pl.DeviceIdType.MESH
CTX = 8
TILE = 16


class Place:
    def __init__(self):
        self.c, self.z = lax.axis_index("ctx"), lax.axis_index("wsh")
        self.core = lax.rem(self.c, 2)
        self.x = lax.rem(self.c // 2, 2)
        self.y = self.c // 4

    def flip(self, core=0, x=0, y=0):
        core = 1 - self.core if core else self.core
        x = 1 - self.x if x else self.x
        y = 1 - self.y if y else self.y
        return core, x, y

    def device(self, **axes):
        core, x, y = self.flip(**axes)
        return (y * 4 + x * 2 + core, self.z)

    def chip(self, **axes):
        core, x, y = self.flip(**axes)
        return y * 2 + x

    def piece(self, **axes):
        core, x, y = self.flip(**axes)
        return core * 4 + y * 2 + x


def greet(me, depth):
    barrier = pltpu.get_barrier_semaphore()
    for axes in ({"core": 1}, {"x": 1}, {"y": 1}):
        pl.semaphore_signal(barrier, inc=1, device_id=me.device(**axes), device_id_type=MESH)

    @pl.when(me.z > 0)
    def _():
        pl.semaphore_signal(barrier, inc=1, device_id=(me.c, me.z - 1), device_id_type=MESH)

    @pl.when(me.z < depth - 1)
    def _():
        pl.semaphore_signal(barrier, inc=1, device_id=(me.c, me.z + 1), device_id_type=MESH)

    line_peers = jnp.where(me.z > 0, 1, 0) + jnp.where(me.z < depth - 1, 1, 0)
    pl.semaphore_wait(barrier, 3 + line_peers)


def remote(src, dst, send, recv, device):
    return pltpu.make_async_remote_copy(
        src_ref=src, dst_ref=dst, send_sem=send, recv_sem=recv, device_id=device, device_id_type=MESH
    )


def rows_at(start, count):
    return pl.ds(pl.multiple_of(start, TILE), count)


def cut(size):
    first = (size // TILE + 1) // 2 * TILE
    return first, size - first


SPREAD = 9
X, Y, XY = {"x": 1}, {"y": 1}, {"x": 1, "y": 1}
CORE = {"core": 1}


def spread(me, size, own, buf, send, recv):
    first, second = cut(size)
    whole, one, two = (0, size), (0, first), (first, second)
    moves = (
        ({}, whole, X),
        ({}, whole, Y),
        ({}, whole, CORE),
        (X, one, Y),
        (X, whole, CORE),
        (Y, two, X),
        (Y, whole, CORE),
        (XY, one, CORE),
        (XY, two, CORE),
    )

    def region(axes, part):
        return buf(me.piece(**axes) * size + part[0], part[1])

    def sent(i):
        axes, part, to = moves[i]
        here = own if not axes else region(axes, part)
        return remote(here, region(axes, part), send(i), recv(i), me.device(**to))

    def arrived(i):
        axes, part, to = moves[i]
        source = {key: 1 for key in ("core", "x", "y") if (key in axes) != (key in to)}
        there = region(source, part)
        remote(there, there, send(i), recv(i), me.device(**to)).wait_recv()

    def begin():
        for i in (0, 1, 2):
            sent(i).start()

    def middle():
        arrived(0)
        sent(3).start()
        sent(4).start()
        arrived(1)
        sent(5).start()
        sent(6).start()

    def late():
        arrived(3)
        sent(7).start()
        arrived(5)
        sent(8).start()

    def finish():
        for i in (2, 4, 6, 7, 8):
            arrived(i)
        for i in range(SPREAD):
            sent(i).wait_send()

    return begin, middle, late, finish


def layout(arrays, lead, width):
    plan, start = [], 0
    for n, array in enumerate(arrays):
        rows = array.shape[0] // lead
        for i in range(array.shape[1] // width):
            plan.append((n, i * width, rows, start))
            start += rows
    return plan, start


def gather_kernel(count, *refs):
    parts, result, out = refs[:count], refs[count], refs[count + 1]
    line_send, line_recv, send, recv, local, stored = refs[count + 2 :]
    depth, total, width = out.shape
    size = total // CTX
    me = Place()
    plan, used = layout(parts, 1, width)
    keeps = [
        pltpu.make_async_copy(
            parts[n].at[:, pl.ds(column, width)], out.at[me.z, pl.ds(start, rows)], local.at[m]
        )
        for m, (n, column, rows, start) in enumerate(plan)
    ]
    for keep in keeps:
        keep.start()
    greet(me, depth)
    for keep in keeps:
        keep.wait()

    def store(origin):
        return pltpu.make_async_copy(out.at[origin], result.at[origin], stored.at[origin])

    mine = rows_at(me.piece() * size, size)

    def along(way, t):
        origin, to = (me.z - t, me.z + 1) if way == 0 else (me.z + t, me.z - 1)
        origin, to = jnp.clip(origin, 0, depth - 1), jnp.clip(to, 0, depth - 1)
        here = out.at[origin, mine]
        pair = (line_send.at[way, t], line_recv.at[way, t])
        return remote(here, out.at[origin, mine], *pair, (me.c, to))

    def goes(way, t):
        if way == 0:
            return (me.z >= t) & (me.z + 1 < depth)
        return (me.z + t < depth) & (me.z >= 1)

    def comes(way, t):
        return me.z >= t if way == 0 else me.z + t < depth

    def steps(way, t):
        origin = jnp.clip(me.z - t if way == 0 else me.z + t, 0, depth - 1)
        slot = way * (depth - 1) + t - 1
        return spread(
            me,
            size,
            out.at[origin, mine],
            lambda start, count: out.at[origin, rows_at(start, count)],
            lambda i: send.at[slot, i],
            lambda i: recv.at[slot, i],
        )

    for way in (0, 1):

        @pl.when(goes(way, 0))
        def _():
            along(way, 0).start()

    store(me.z).start()
    for t in range(1, depth + 2):
        for way in (0, 1):
            if t < depth:

                @pl.when(comes(way, t))
                def _():
                    origin = jnp.clip(me.z - t if way == 0 else me.z + t, 0, depth - 1)
                    there = out.at[origin, mine]
                    pair = (line_send.at[way, t - 1], line_recv.at[way, t - 1])
                    remote(there, there, *pair, me.device(**X)).wait_recv()
                    if t < depth - 1:

                        @pl.when(goes(way, t))
                        def _():
                            along(way, t).start()

                    steps(way, t)[0]()

        for way in (0, 1):
            if 1 <= t - 1 < depth:

                @pl.when(comes(way, t - 1))
                def _():
                    steps(way, t - 1)[1]()

        for way in (0, 1):
            if 1 <= t - 2 < depth:

                @pl.when(comes(way, t - 2))
                def _():
                    steps(way, t - 2)[2]()

    for way in (0, 1):
        for t in range(1, depth):

            @pl.when(comes(way, t))
            def _():
                steps(way, t)[3]()
                store(jnp.clip(me.z - t if way == 0 else me.z + t, 0, depth - 1)).start()

        for t in range(depth - 1):

            @pl.when(goes(way, t))
            def _():
                along(way, t).wait_send()

    for zz in range(depth):
        store(zz).wait()


def gather_packed(parts, width):
    depth = lax.axis_size("wsh")
    dma = pltpu.SemaphoreType.DMA
    plan, used = layout(parts, 1, width)
    return pl.pallas_call(
        functools.partial(gather_kernel, len(parts)),
        out_shape=jax.ShapeDtypeStruct((depth, used, width), parts[0].dtype),
        in_specs=[pl.BlockSpec(memory_space=pl.ANY)] * len(parts),
        out_specs=pl.BlockSpec(memory_space=pl.ANY),
        scratch_shapes=[
            pltpu.VMEM((depth, used, width), parts[0].dtype),
            dma((2, depth - 1)),
            dma((2, depth - 1)),
            dma((2 * (depth - 1), SPREAD)),
            dma((2 * (depth - 1), SPREAD)),
            dma((len(plan),)),
            dma((depth,)),
        ],
        compiler_params=pltpu.CompilerParams(
            collective_id=1, has_side_effects=True, vmem_limit_bytes=32 * 2**20
        ),
    )(*parts)


def add_rows(total, start, terms, count):
    def body(i, carry):
        at = rows_at(start + i * TILE, TILE)
        value = total[at, :].astype(jnp.float32)
        for ref, base in terms:
            value = value + ref[rows_at(base + i * TILE, TILE), :].astype(jnp.float32)
        total[at, :] = value.astype(total.dtype)
        return carry

    lax.fori_loop(0, count // TILE, body, 0)


def reduce_kernel(count, *refs):
    parts, out = refs[:count], refs[count]
    total, pair, near_x, near_y, last, line = refs[count + 1 : count + 7]
    local, core_send, core_recv, near_send, near_recv = refs[count + 7 : count + 12]
    line_send, line_recv, send, recv, keep_sem = refs[count + 12 :]
    depth, size, width = last.shape
    half = 4 * size
    first, second = cut(size)
    me = Place()
    k, kx, ky, kd = me.chip(), me.chip(**X), me.chip(**Y), me.chip(**XY)
    to_x, to_y, to_core = me.device(**X), me.device(**Y), me.device(**CORE)

    def cores(zz):
        return remote(
            total.at[zz, rows_at((1 - me.core) * half, half)],
            pair.at[zz],
            core_send.at[zz],
            core_recv.at[zz],
            to_core,
        )

    plan, used = layout(parts, depth, width)
    base = me.core * half

    def own(zz):
        return [
            pltpu.make_async_copy(
                parts[n].at[pl.ds(zz * rows, rows), pl.ds(column, width)],
                total.at[zz, pl.ds(start, rows)],
                local.at[zz, m],
            )
            for m, (n, column, rows, start) in enumerate(plan)
        ]

    def near(zz, i):
        sems = (near_send.at[zz, i], near_recv.at[zz, i])
        part = lambda chip, offset, count: total.at[zz, rows_at(base + chip * size + offset, count)]
        if i == 0:
            return remote(part(kd, 0, first), near_x.at[zz, 1], *sems, to_x)
        if i == 1:
            return remote(part(kd, first, second), near_y.at[zz, 1], *sems, to_y)
        if i == 2:
            return remote(part(kx, 0, first), near_x.at[zz, 0], *sems, to_x)
        if i == 3:
            return remote(part(ky, first, second), near_y.at[zz, 0], *sems, to_y)
        if i == 4:
            return remote(part(ky, 0, first), last.at[zz, pl.ds(0, first)], *sems, to_y)
        return remote(part(kx, first, second), last.at[zz, pl.ds(first, second)], *sems, to_x)

    for zz in range(depth):
        for copy in own(zz):
            copy.start()
    greet(me, depth)
    for zz in range(depth):
        for copy in own(zz):
            copy.wait()
        cores(zz).start()
    for t in range(depth + 2):
        if t < depth:
            cores(t).wait_recv()
            add_rows(total.at[t], base, [(pair.at[t], 0)], half)
            for i in range(4):
                near(t, i).start()
        if 0 <= t - 1 < depth:
            zz = t - 1
            near(zz, 0).wait_recv()
            add_rows(total.at[zz], base + ky * size, [(near_x.at[zz, 1], 0)], first)
            near(zz, 4).start()
            near(zz, 1).wait_recv()
            add_rows(total.at[zz], base + kx * size + first, [(near_y.at[zz, 1], 0)], second)
            near(zz, 5).start()
        if 0 <= t - 2 < depth:
            zz = t - 2
            near(zz, 2).wait_recv()
            near(zz, 4).wait_recv()
            add_rows(total.at[zz], base + k * size, [(near_x.at[zz, 0], 0), (last.at[zz], 0)], first)
            near(zz, 3).wait_recv()
            near(zz, 5).wait_recv()
            terms = [(near_y.at[zz, 0], 0), (last.at[zz], first)]
            add_rows(total.at[zz], base + k * size + first, terms, second)

    mine = rows_at(base + k * size, size)

    def along(way, zz):
        to = jnp.clip(me.z - 1 if way == 0 else me.z + 1, 0, depth - 1)
        sems = (line_send.at[way, zz], line_recv.at[way, zz])
        return remote(total.at[zz, mine], line.at[way, zz], *sems, (me.c, to))

    def goes(way, zz):
        return zz < me.z if way == 0 else zz > me.z

    def fed(way):
        return me.z + 1 < depth if way == 0 else me.z >= 1

    def take(way, zz):
        @pl.when(fed(way))
        def _():
            along(way, zz).wait_recv()
            add_rows(total.at[zz], base + k * size, [(line.at[way, zz], 0)], size)

    for j in range(depth):
        for way, zz in ((0, j), (1, depth - 1 - j)):

            @pl.when(goes(way, zz))
            def _():
                take(way, zz)
                along(way, zz).start()

    take(0, me.z)
    take(1, me.z)
    done = total.at[me.z, mine]
    begin, middle, late, finish = spread(
        me,
        size,
        done,
        lambda start, count: out.at[rows_at(start, count)],
        lambda i: send.at[i],
        lambda i: recv.at[i],
    )
    begin()
    keep = pltpu.make_async_copy(done, out.at[rows_at(me.piece() * size, size)], keep_sem)
    keep.start()
    middle()
    late()
    finish()
    keep.wait()
    for zz in range(depth):
        cores(zz).wait_send()
        for i in range(6):
            near(zz, i).wait_send()
        for way in (0, 1):

            @pl.when(goes(way, zz))
            def _():
                along(way, zz).wait_send()


def reduce_packed(parts, width):
    depth = lax.axis_size("wsh")
    plan, rows = layout(parts, depth, width)
    size = rows // CTX
    first, second = cut(size)
    dma = pltpu.SemaphoreType.DMA
    low = parts[0].dtype
    return pl.pallas_call(
        functools.partial(reduce_kernel, len(parts)),
        out_shape=jax.ShapeDtypeStruct((rows, width), low),
        in_specs=[pl.BlockSpec(memory_space=pl.ANY)] * len(parts),
        out_specs=pl.BlockSpec(memory_space=pl.ANY),
        scratch_shapes=[
            pltpu.VMEM((depth, rows, width), low),
            pltpu.VMEM((depth, 4 * size, width), low),
            pltpu.VMEM((depth, 2, first, width), low),
            pltpu.VMEM((depth, 2, second, width), low),
            pltpu.VMEM((depth, size, width), low),
            pltpu.VMEM((2, depth, size, width), low),
            dma((depth, len(plan))),
            dma((depth,)),
            dma((depth,)),
            dma((depth, 6)),
            dma((depth, 6)),
            dma((2, depth)),
            dma((2, depth)),
            dma((SPREAD,)),
            dma((SPREAD,)),
            dma,
        ],
        compiler_params=pltpu.CompilerParams(
            collective_id=2, has_side_effects=True, vmem_limit_bytes=48 * 2**20
        ),
    )(*parts)


def spare_rows(used):
    step = CTX * TILE
    return (used + 2 + step - 1) // step * step - used


def by_heads(tokens, key_mask, w_qkv, w_attn_out, w_in, w_out, attn_gain, mlp_gain, cotangent):
    seqs, rows, width = tokens.shape
    peers = lax.axis_size("ctx")
    head_width = width // HEADS
    half = head_width // 2
    pairs = seqs * HEADS // peers
    splits = peers // seqs
    feats = pairs * head_width
    length = rows * peers
    tokens_here = seqs * rows
    low = jnp.bfloat16

    depth = lax.axis_size("wsh")
    share, shape_out = w_qkv.shape[0], w_out.shape
    blocks = w_qkv.shape[1] // width
    blocks_in = w_in.shape[1] // width

    used = (blocks + 1 + blocks_in) * share + shape_out[0]
    spare = spare_rows(used)
    gain_rows = jnp.pad(
        jnp.stack([attn_gain, mlp_gain]), ((0, spare - 2), (0, width - share))
    )
    packed = gather_packed([w_qkv, w_attn_out, w_in, w_out, gain_rows], width)

    def unfold(start, rows_each, count):
        return jnp.concatenate(
            [
                packed[:, start + i * rows_each : start + (i + 1) * rows_each].reshape(-1, width)
                for i in range(count)
            ],
            axis=1,
        )

    at_attn = blocks * share
    at_in = at_attn + share
    at_out = at_in + blocks_in * share
    at_gain = at_out + shape_out[0]
    full_qkv = unfold(0, share, blocks)
    full_attn = unfold(at_attn, share, 1)
    full_in = unfold(at_in, share, blocks_in)
    full_out = unfold(at_out, shape_out[0], 1)
    gain_one = packed[:, at_gain, :share].reshape(-1)
    gain_two = packed[:, at_gain + 1, :share].reshape(-1)

    def to_heads(parts):
        count = parts.shape[0]
        sent = jnp.transpose(
            parts.reshape(count, splits, feats, seqs, rows), (3, 1, 0, 2, 4)
        ).reshape(peers, count * feats, rows)
        return sent

    def swap(sent):
        return lax.all_to_all(sent, "ctx", split_axis=0, concat_axis=0, tiled=True)

    def to_rows(parts):
        count = parts.shape[0]
        sent = jnp.transpose(
            parts.astype(low).reshape(count * feats, peers, rows), (1, 0, 2)
        )
        got = swap(sent).reshape(seqs, splits, count, feats, rows)
        return jnp.transpose(got, (2, 1, 3, 0, 4)).reshape(count, width, tokens_here)

    residual_in = tokens.reshape(tokens_here, width).astype(jnp.float32)
    normed_f, norm_one_pull = jax.vjp(layer_norm, residual_in, gain_one.astype(jnp.float32))
    normed = normed_f.astype(low)
    joined = mm(full_qkv, normed, (((0,), (1,)), ((), ())))

    local_pos = lax.axis_index("ctx") * rows + jnp.arange(rows, dtype=jnp.int32)
    inverse = jnp.exp(
        jnp.arange(half, dtype=jnp.float32) * (-2.0 * math.log(THETA) / head_width)
    )
    angles = inverse[:, None] * jnp.tile(local_pos, seqs).astype(jnp.float32)[None, :]
    cosine, sine = jnp.cos(angles), jnp.sin(angles)

    def turn(values, way):
        pair = values.reshape(HEADS, 2, half, tokens_here)
        first, second = pair[:, 0], pair[:, 1]
        return jnp.stack(
            [first * cosine - way * (second * sine), second * cosine + way * (first * sine)], axis=1
        ).reshape(width, tokens_here)

    trio = jnp.stack(
        [turn(joined[:width], 1.0), turn(joined[width : 2 * width], 1.0), joined[2 * width :]]
    ).astype(low)
    mask_rows = jnp.broadcast_to(
        key_mask.astype(low)[:, None, None, :], (seqs, splits, 16, rows)
    ).reshape(peers, 16, rows)
    got = swap(jnp.concatenate([to_heads(trio), mask_rows], axis=1))
    got = jnp.transpose(got, (1, 0, 2)).reshape(3 * feats + 16, length)
    queries, keys, values = (
        got[i * feats : (i + 1) * feats].reshape(pairs, head_width, length) for i in range(3)
    )
    mask_col = got[3 * feats].astype(jnp.float32)[:, None]
    mixed, prob = attend(queries, keys, values, mask_col)
    attended = jnp.transpose(to_rows(mixed.reshape(1, feats, length))[0])

    hidden = residual_in + mm(attended, full_attn)
    normed_two_f, norm_two_pull = jax.vjp(layer_norm, hidden, gain_two.astype(jnp.float32))
    normed_two = normed_two_f.astype(low)
    projected = mm(normed_two, full_in)
    gated_f, glu_pull = jax.vjp(geglu, projected)
    gated = gated_f.astype(low)
    outcome = (hidden + mm(gated, full_out)).astype(low).reshape(seqs, rows, width)
    grad_out = cotangent.reshape(tokens_here, width)
    term_out = mm(gated, grad_out, TN).astype(low)
    (grad_proj,) = glu_pull(mm(grad_out, full_out, NT))
    grad_proj = grad_proj.astype(low)
    term_in = mm(normed_two, grad_proj, TN).astype(low)
    grad_hidden_ln, grad_gain_two = norm_two_pull(mm(grad_proj, full_in, NT))
    grad_hidden = grad_out.astype(jnp.float32) + grad_hidden_ln
    grad_branch = grad_hidden.astype(low)
    term_attn = mm(attended, grad_branch, TN).astype(low)
    grad_att = mm(full_attn, grad_branch, NT).astype(low)
    got_do = swap(to_heads(grad_att[None]))
    got_do = jnp.transpose(got_do, (1, 0, 2)).reshape(pairs, head_width, length)
    grads = attend_back(queries, keys, values, got_do, mixed, prob)
    back = to_rows(jnp.stack([g.reshape(feats, length) for g in grads])).astype(jnp.float32)
    grad_joined = jnp.concatenate([turn(back[0], -1.0), turn(back[1], -1.0), back[2]]).astype(low)
    term_qkv = mm(normed, grad_joined, (((0,), (1,)), ((), ()))).astype(low)
    grad_normed = mm(grad_joined, full_qkv, (((0,), (1,)), ((), ())))
    grad_in_ln, grad_gain_one = norm_one_pull(grad_normed)
    grad_tokens = (grad_hidden + grad_in_ln).astype(low).reshape(seqs, rows, width)
    gain_terms = jnp.stack([grad_gain_one, grad_gain_two]).astype(low)
    gain_terms = jnp.transpose(gain_terms.reshape(2, depth, share), (1, 0, 2))

    gain_terms = jnp.pad(gain_terms, ((0, 0), (0, spare - 2), (0, width - share)))
    terms = [term_qkv, term_attn, term_in, term_out, gain_terms.reshape(-1, width)]
    sums = reduce_packed(terms, width).astype(jnp.float32)

    def side(start, count):
        return jnp.concatenate(
            [sums[start + i * share : start + (i + 1) * share] for i in range(count)], axis=1
        )

    return (
        outcome,
        grad_tokens,
        sums[at_gain, :share],
        sums[at_gain + 1, :share],
        side(0, blocks),
        side(at_attn, 1),
        side(at_in, blocks_in),
        sums[at_out : at_out + shape_out[0]],
    )


def shards(*arrays):
    seqs = arrays[0].shape[0]
    peers = lax.axis_size("ctx")
    even = (seqs * HEADS) % peers == 0 and peers % seqs == 0 and peers == CTX
    even = even and lax.axis_size("wsh") > 1 and arrays[4].shape[1] % arrays[0].shape[2] == 0
    return (by_heads if even else by_positions)(*arrays)


def solution(mesh):
    return jax.shard_map(
        shards,
        mesh=mesh,
        in_specs=(
            P("wsh", "ctx", None),
            P("wsh", "ctx"),
            P("wsh", None),
            P("wsh", None),
            P("wsh", None),
            P("wsh", None),
            P("wsh"),
            P("wsh"),
            P("wsh", "ctx", None),
        ),
        out_specs=(
            P("wsh", "ctx", None),
            P("wsh", "ctx", None),
            P("wsh"),
            P("wsh"),
            P("wsh", None),
            P("wsh", None),
            P("wsh", None),
            P("wsh", None),
        ),
        check_vma=False,
    )
```
